256 devices in a mesh: section: 4 (over y), tp: 64 (over x, z, core).
Axes of the slice: x: 4, y: 4, z: 8, core: 2. Of those that a mesh axis runs over, the one named last changes fastest.
Arguments:
- tokens: bfloat16 [16, 64, 5120], P('section', None, 'tp'), may hold values from -6 to 6
- language: int32 [16, 1], P('section'), may hold values from 0 to 3; in each aligned block of 4 rows (0 to 3, 4 to 7, ...) at most 2 rows name the same one
- example_ids: int32 [16], P('section'), may hold values from 0 to 15, each once
- history: bfloat16 [16, 64, 5120], P(None, None, 'tp'), may hold values from -6 to 6
- enc_gain: float32 [5120], replicated, may hold values from 0.1 to 1.9
- dec_gain: float32 [4, 5120], P('section'), may hold values from 0.1 to 1.9
- enc_gate: bfloat16 [5120, 20480], P('section', 'tp'), may hold values from -0.078125 to 0.078125
- enc_in: bfloat16 [5120, 20480], P('section', 'tp'), may hold values from -0.078125 to 0.078125
- enc_out: bfloat16 [20480, 5120], P('tp', 'section'), may hold values from -0.0390625 to 0.0390625
- dec_gate: bfloat16 [4, 5120, 20480], P('section', None, 'tp'), may hold values from -0.078125 to 0.078125
- dec_in: bfloat16 [4, 5120, 20480], P('section', None, 'tp'), may hold values from -0.078125 to 0.078125
- dec_out: bfloat16 [4, 20480, 5120], P('section', 'tp'), may hold values from -0.0390625 to 0.0390625
Outputs:
- decoded: bfloat16 [16, 64, 5120], P('section', None, 'tp')
- new_memory: bfloat16 [16, 64, 5120], P('section', None, 'tp')
- quantized: bfloat16 [16, 64, 5120], P('section', None, 'tp')
The draws below stay inside these ranges and needn't reach their ends.
Inputs may be any that keep to these rules, and one draw needn't show every extreme that they name: In each aligned block of 4 examples (those of one section group) no language is named by more than 2 examples, a bound that some block reaches. `example_ids`: every buffer row is named by exactly one example.
All inputs are finite; a program needn't handle non-finite values. Where the reference program divides by a largest or mean magnitude, that divisor is 1e-20 or more.
Results may differ from the reference program's by a relative error of at most 0.015.
Values may be sent and summed in bfloat16 or wider, within the bound.
A program may use at most 128 MiB of HBM per device.

```python
import math
import jax
import jax.numpy as jnp
import numpy as np
from jax import lax

D = 5120
FF = 20480
SEQ = 64
EX_DEV = 4
CAP = 2
EXAMPLES = 16
N_SECTION = 4


def block_levels(stream_key, shape, split, smallest, largest):
    def one(position, shards_of):
        steps = jax.random.uniform(jax.random.fold_in(jax.random.fold_in(stream_key, 6), position), (shards_of,), jnp.float32, smallest / len(split), largest / len(split))
        return jnp.repeat(jnp.exp(steps), shape[position] // shards_of).reshape((-1,) + (1,) * (len(shape) - position - 1))

    factor_of = one(*split[0])
    for cut in split[1:]:
        factor_of = factor_of * one(*cut)
    return factor_of


def shared_out(rng, own, number, rows, number_of, top, reach, slope):
    ranking = jax.random.permutation(rng, number_of)
    packed, ordinary = load_shares(number_of, rows * top, reach, slope, True), load_shares(number_of, rows * top, reach, slope, False)
    places = jnp.arange(number_of)

    def named(sizes, rotation):
        used = int((sizes > 0).sum())
        fixed = max(1, used // 4)
        shifted = fixed + (places - fixed + rotation * (used - fixed)) % max(1, number_of - fixed)
        return jnp.zeros((number_of,), jnp.int32).at[ranking[jnp.where(places < fixed, places, shifted)]].set(jnp.asarray(sizes, jnp.int32))

    sizes = jnp.where(number % 4 == 0, named(packed, number // 4), named(ordinary, number - number // 4 - 1))
    mixed = jax.random.permutation(jax.random.fold_in(own, 3), number_of)
    donor, sink = mixed[0:number_of // 2 * 2:2], mixed[1:number_of // 2 * 2:2]
    slack = jnp.minimum(sizes[donor] - 1, reach - sizes[sink]) // 2
    slack = jnp.where((donor == ranking[0]) | (sink == ranking[0]) | (sizes[sink] == 0), 0, jnp.maximum(slack, 0))
    shifted = jax.random.randint(jax.random.fold_in(own, 4), (number_of // 2,), 0, 1 << 20) % (slack + 1)
    sizes = sizes.at[donor].add(-shifted).at[sink].add(shifted)
    labels = jnp.searchsorted(jnp.cumsum(sizes), jnp.arange(rows * top), side="right").astype(jnp.int32)
    table = labels.reshape(top, rows).T
    table = table[jax.random.permutation(jax.random.fold_in(own, 1), rows)]
    rotation = jax.random.randint(jax.random.fold_in(own, 2), (rows, 1), 0, top)
    return jnp.take_along_axis(table, (jnp.arange(top)[None, :] + rotation) % top, axis=1)


def load_shares(count, total, reach, skew, full):
    portions = [(1 << 20) // math.isqrt(standing ** skew) + 1 for standing in range(1, count + 1)]
    largest = reach if full else min(reach, max(-(-total // count), total * portions[0] // sum(portions)))
    least = 1 if total - largest >= count - 1 else 0
    given, surplus = [largest] + [least] * (count - 1), total - largest - least * (count - 1)
    while surplus > 0:
        candidates = [i for i in range(1, count) if given[i] < largest] or [i for i in range(1, count) if given[i] < reach]
        pool, budget = sum([portions[i] for i in candidates]), surplus
        for i in candidates:
            addition = min(reach - given[i], max(1, budget * portions[i] // pool), surplus)
            given[i] = given[i] + addition
            surplus = surplus - addition
    return np.array(given)


def bell_draw(own_key, dims, spread, limit, split=(), dtype=jnp.bfloat16):
    result = jax.random.normal(own_key, dims, jnp.float32) * spread
    if len(split) > 0:
        result = block_levels(own_key, dims, split, -0.22, 0.18) * result
    return jnp.clip(result, min=-limit, max=limit).astype(dtype)


def setup_inputs(seed: int = 0) -> dict:
    key_of = jax.random.split(jax.random.key(seed), 13)
    tokens = bell_draw(key_of[0], (EXAMPLES, SEQ, D), 1.0, 6.0, ((0, 4), (2, 64)))
    language_keys = jax.random.split(jax.random.fold_in(key_of[1], 1), EXAMPLES // EX_DEV)
    language_turns = jax.random.permutation(jax.random.fold_in(key_of[1], 3), EXAMPLES // EX_DEV)
    language = jax.vmap(lambda own, number: shared_out(jax.random.fold_in(key_of[1], 2), own, number, EX_DEV, N_SECTION, 1, CAP, 2))(language_keys, language_turns).reshape((EXAMPLES, 1))
    example_ids = jax.random.permutation(key_of[2], EXAMPLES).astype(jnp.int32)
    history = bell_draw(key_of[3], (EXAMPLES, SEQ, D), 1.0, 6.0, ((2, 64),))
    enc_gain = jnp.clip(1.0 + 0.18 * jax.random.normal(key_of[4], (D,), jnp.float32), 0.1, 1.9)
    dec_gain = jnp.clip(1.0 + 0.18 * jax.random.normal(key_of[5], (N_SECTION, D), jnp.float32), 0.1, 1.9)
    enc_gate = bell_draw(key_of[6], (D, FF), D ** -0.5, 0.078125, ((0, 4), (1, 64)))
    enc_in = bell_draw(key_of[7], (D, FF), D ** -0.5, 0.078125, ((0, 4), (1, 64)))
    enc_out = bell_draw(key_of[8], (FF, D), FF ** -0.5, 0.0390625, ((0, 64), (1, 4)))
    dec_gate = bell_draw(key_of[9], (N_SECTION, D, FF), D ** -0.5, 0.078125, ((0, 4), (2, 64)))
    dec_in = bell_draw(key_of[10], (N_SECTION, D, FF), D ** -0.5, 0.078125, ((0, 4), (2, 64)))
    dec_out = bell_draw(key_of[11], (N_SECTION, FF, D), FF ** -0.5, 0.0390625, ((0, 4), (1, 64)))
    return dict(tokens=tokens, language=language, example_ids=example_ids, history=history, enc_gain=enc_gain, dec_gain=dec_gain, enc_gate=enc_gate, enc_in=enc_in, enc_out=enc_out, dec_gate=dec_gate, dec_in=dec_in, dec_out=dec_out)


epsilon = 1e-06

def rms_norm(values, gain):
    wide = values.astype(jnp.float32)
    return wide * lax.rsqrt(lax.optimization_barrier(jnp.mean(wide * wide, axis=-1, keepdims=True)) + epsilon) * gain

def reference(tokens, language, example_ids, history, enc_gain, dec_gain, enc_gate, enc_in, enc_out, dec_gate, dec_in, dec_out):
    flattened = tokens.reshape(EXAMPLES * SEQ, D)
    normed = rms_norm(flattened, enc_gain).astype(jnp.bfloat16)
    pre_gate = jnp.dot(normed, enc_gate, preferred_element_type=jnp.float32)
    pre_up = jnp.dot(normed, enc_in, preferred_element_type=jnp.float32)
    hidden = (jax.nn.gelu(pre_gate) * pre_up).astype(jnp.bfloat16)
    encoded = (flattened.astype(jnp.float32) + jnp.dot(hidden, enc_out, preferred_element_type=jnp.float32)).astype(jnp.bfloat16)
    encoded = encoded.reshape(EXAMPLES, SEQ, D)
    baseline = jnp.take(history, example_ids.astype(jnp.int32), axis=0)
    difference = encoded.astype(jnp.float32) - baseline.astype(jnp.float32)
    block_scale = lax.optimization_barrier(jnp.max(jnp.abs(difference), axis=1, keepdims=True)) + epsilon
    quantized = (difference / block_scale).astype(jnp.bfloat16)
    new_memory = (baseline.astype(jnp.float32) + quantized.astype(jnp.float32) * block_scale).astype(jnp.bfloat16)

    def decode(pair):
        example, lang_index = pair
        dec_normed = rms_norm(example, dec_gain[lang_index]).astype(jnp.bfloat16)
        gate_part = jnp.dot(dec_normed, dec_gate[lang_index], preferred_element_type=jnp.float32)
        up_part = jnp.dot(dec_normed, dec_in[lang_index], preferred_element_type=jnp.float32)
        dec_hidden = (jax.nn.gelu(gate_part) * up_part).astype(jnp.bfloat16)
        summed = jnp.dot(dec_hidden, dec_out[lang_index], preferred_element_type=jnp.float32)
        return (example.astype(jnp.float32) + summed).astype(jnp.bfloat16)
    decoded = lax.map(decode, (new_memory, language[:, 0].astype(jnp.int32)))
    return (decoded, new_memory, quantized)
```

```python
import functools

import jax
import jax.numpy as jnp
from jax import lax
from jax.experimental import pallas as pl
from jax.experimental.pallas import tpu as pltpu
from jax.sharding import PartitionSpec as P

MESH = pl.DeviceIdType.MESH
BF16 = jnp.bfloat16
F32 = jnp.float32
EPS = 1e-06
NX, NZ, NY = 4, 8, 4
SEQ = 64
PART = 80
HEAD = 48
TAIL = PART - HEAD
SLICE = 1280
UNITS = 320
WIDTH = 5120
COPIES = 112


class Links:
    def __init__(self, send_sem, recv_sem):
        self.send_sem, self.recv_sem = send_sem, recv_sem
        self.count = 0
        self.sent = []

    def start(self, src, dst, device):
        copy = pltpu.make_async_remote_copy(
            src_ref=src,
            dst_ref=dst,
            send_sem=self.send_sem.at[self.count],
            recv_sem=self.recv_sem.at[self.count],
            device_id=device,
            device_id_type=MESH,
        )
        self.count += 1
        copy.start()
        self.sent.append(copy)
        return copy

    def finish(self):
        for copy in self.sent:
            copy.wait_send()
        self.sent = []


class Place:
    def __init__(self):
        self.y = lax.axis_index("section")
        t = lax.axis_index("tp")
        self.x, self.z, self.c = t // 16, (t // 2) % 8, t % 2
        self.d = 1 - 2 * self.c

    def at(self, y=None, x=None, z=None, c=None):
        y = self.y if y is None else y
        x = self.x if x is None else x
        z = self.z if z is None else z
        c = self.c if c is None else c
        return (y, (x * 8 + z) * 2 + c)

    def xo(self, off):
        return (self.x + off + 8) % 4

    def yo(self, off):
        return (self.y + off + 8) % 4

    def zo(self, off):
        return (self.z + self.d * off + 16) % 8

    def plane(self):
        return [
            self.at(z=self.zo(1)),
            self.at(z=self.zo(-1)),
            self.at(x=self.xo(1)),
            self.at(x=self.xo(-1)),
            self.at(c=1 - self.c),
        ]

    def column(self):
        return [self.at(y=self.yo(k)) for k in (1, 2, 3)]


ORDER = (0, -1, 1, -2, 2, -3, 3, -4)
TARGETS = (4, -3, 3, -2, 2, -1, 1, 0)


def gather_plane(links, me, blocks):
    zp, zm, xp, xm, partner = me.plane()
    x, z, c = me.x, me.z, me.c

    def head(xx, off):
        return blocks.at[xx, me.zo(off), c, pl.ds(0, HEAD)]

    def tail(xx):
        return blocks.at[xx, z, c, pl.ds(HEAD, TAIL)]

    def heads(off):
        return blocks.at[:, me.zo(off), c, pl.ds(0, HEAD)]

    def tails(off):
        return blocks.at[:, me.zo(off), c, pl.ds(HEAD, TAIL)]

    along, tail_along, cross, second, core = {}, {}, {}, {}, []

    def head_z(off):
        if -4 < off <= 0:
            along[off - 1] = links.start(head(x, off), head(x, off), zp)
        if 0 <= off < 3:
            along[off + 1] = links.start(head(x, off), head(x, off), zm)

    def head_x(off):
        cross[off] = (
            links.start(head(x, off), head(x, off), xp),
            links.start(head(x, off), head(x, off), xm),
        )

    def tail_z(off):
        if -4 < off <= 0:
            tail_along[off - 1] = links.start(tails(off), tails(off), zp)
        if 0 <= off < 3:
            tail_along[off + 1] = links.start(tails(off), tails(off), zm)

    def to_core(ref):
        core.append(links.start(ref, ref, partner))

    def hop(index):
        off = ORDER[index]
        cross[off][0].wait_recv()
        cross[off][1].wait_recv()
        if index % 2 == 0:
            second[off] = links.start(head(me.xo(-1), off), head(me.xo(-1), off), xp)
        else:
            second[off] = links.start(head(me.xo(1), off), head(me.xo(1), off), xm)

    def land(index):
        off = ORDER[index]
        second[off].wait_recv()
        to_core(heads(off))

    def tail_step(index):
        off = ORDER[index]
        tail_along[off].wait_recv()
        tail_z(off)
        to_core(tails(off))

    head_z(0)
    tail_x = (links.start(tail(x), tail(x), xp), links.start(tail(x), tail(x), xm))
    head_x(0)
    for i in range(1, 8):
        off = ORDER[i]
        along[off].wait_recv()
        head_z(off)
        head_x(off)
        if i == 1:
            tail_x[0].wait_recv()
            tail_x[1].wait_recv()
            onward = tail(me.xo(-me.d))
            tail_second = links.start(onward, onward, me.at(x=me.xo(me.d)))
        if i == 2:
            tail_second.wait_recv()
            tail_z(0)
            to_core(tails(0))
        if i >= 4:
            tail_step(i - 3)
        hop(i - 1)
        if i >= 2:
            land(i - 2)
    hop(7)
    tail_step(5)
    land(6)
    tail_step(6)
    land(7)
    tail_step(7)
    for copy in core:
        copy.wait_recv()


def add_to(dst, *terms):
    total = dst[...].astype(F32)
    for term in terms:
        total = total + term[...].astype(F32)
    dst[...] = total.astype(dst.dtype)


def scatter_shapes(rows):
    return [
        pltpu.VMEM((NX, NZ, 2, PART, rows), BF16),
        pltpu.VMEM((NX, NZ, PART, rows), BF16),
        pltpu.VMEM((8, HEAD, rows), BF16),
        pltpu.VMEM((8, 2, HEAD, rows), BF16),
        pltpu.VMEM((4, HEAD, rows), BF16),
        pltpu.VMEM((3, HEAD, rows), BF16),
        pltpu.VMEM((4, NX, TAIL, rows), BF16),
        pltpu.VMEM((3, NX, TAIL, rows), BF16),
        pltpu.VMEM((TAIL, rows), BF16),
        pltpu.VMEM((2, TAIL, rows), BF16),
        pltpu.VMEM((PART, rows), F32),
    ]


def scatter_plane(links, me, bufs, core_copies):
    sums, theirs, first, both, up_z, down_z, up_tail, down_tail, tail_first, tail_both, result = bufs
    zp, zm, xp, xm, _ = me.plane()
    x, z, c, d = me.x, me.z, me.c, me.d

    def head(xx, off):
        return sums.at[xx, me.zo(off), c, pl.ds(0, HEAD)]

    def tail(xx):
        return sums.at[xx, z, c, pl.ds(HEAD, TAIL)]

    def tails(off):
        return sums.at[:, me.zo(off), c, pl.ds(HEAD, TAIL)]

    for xx, copy in core_copies:
        copy.wait_recv()
        add_to(sums.at[xx, :, c], theirs.at[xx])

    hops, direct, relayed, along, tail_along = {}, {}, {}, {}, {}
    for i, off in enumerate(TARGETS):
        e = 1 if i % 2 == 0 else -1
        ahead, behind = (xp, xm) if e == 1 else (xm, xp)
        hops[i] = links.start(head(me.xo(2), off), first.at[i], ahead)
        direct[i] = links.start(head(me.xo(-e), off), both.at[i, 1], behind)
        if i == 0:
            tail_along[4] = links.start(tails(4), up_tail.at[0], zp)
            tail_along[-3] = links.start(tails(-3), down_tail.at[0], zm)

    def relay(i):
        off = TARGETS[i]
        e = 1 if i % 2 == 0 else -1
        hops[i].wait_recv()
        add_to(head(me.xo(e), off), first.at[i])
        relayed[i] = links.start(head(me.xo(e), off), both.at[i, 0], xp if e == 1 else xm)

    def tail_step(off):
        if off > 0:
            tail_along[off + 1].wait_recv()
            add_to(tails(off), up_tail.at[3 - off])
            tail_along[off] = links.start(tails(off), up_tail.at[4 - off], zp)
        else:
            tail_along[off - 1].wait_recv()
            add_to(tails(off), down_tail.at[2 + off])
            tail_along[off] = links.start(tails(off), down_tail.at[3 + off], zm)

    def collect(i):
        off = TARGETS[i]
        relayed[i].wait_recv()
        direct[i].wait_recv()
        if off == 4:
            add_to(head(x, off), both.at[i, 0], both.at[i, 1])
            along[4] = links.start(head(x, off), up_z.at[0], zp)
        elif off == -3:
            add_to(head(x, off), both.at[i, 0], both.at[i, 1])
            along[-3] = links.start(head(x, off), down_z.at[0], zm)
        elif off > 0:
            along[off + 1].wait_recv()
            add_to(head(x, off), both.at[i, 0], both.at[i, 1], up_z.at[3 - off])
            along[off] = links.start(head(x, off), up_z.at[4 - off], zp)
        elif off < 0:
            along[off - 1].wait_recv()
            add_to(head(x, off), both.at[i, 0], both.at[i, 1], down_z.at[2 + off])
            along[off] = links.start(head(x, off), down_z.at[3 + off], zm)

    relay(0)
    relay(1)
    for i in range(2, 8):
        relay(i)
        if i < 7:
            tail_step(TARGETS[i])
        collect(i - 2)
    tail_along[1].wait_recv()
    tail_along[-1].wait_recv()
    add_to(tails(0), up_tail.at[3], down_tail.at[2])
    tail_hop = links.start(tail(me.xo(2)), tail_first, me.at(x=me.xo(d)))
    tail_direct = links.start(tail(me.xo(-d)), tail_both.at[1], me.at(x=me.xo(-d)))
    collect(6)
    tail_hop.wait_recv()
    add_to(tail(me.xo(d)), tail_first)
    tail_relayed = links.start(tail(me.xo(d)), tail_both.at[0], me.at(x=me.xo(d)))
    relayed[7].wait_recv()
    direct[7].wait_recv()
    along[1].wait_recv()
    along[-1].wait_recv()
    result[pl.ds(0, HEAD)] = (
        head(x, 0)[...].astype(F32)
        + both[7, 0].astype(F32)
        + both[7, 1].astype(F32)
        + up_z[3].astype(F32)
        + down_z[2].astype(F32)
    )
    tail_relayed.wait_recv()
    tail_direct.wait_recv()
    result[pl.ds(HEAD, TAIL)] = (
        tail(x)[...].astype(F32) + tail_both[0].astype(F32) + tail_both[1].astype(F32)
    )


def contract(a, b):
    return lax.dot_general(a, b, (((0,), (0,)), ((), ())), preferred_element_type=F32)


def gelu(v):
    return jax.nn.gelu(v)


def scale_rows(weights, gain_ref, first_row, count):
    def step(i, carry):
        rows = pl.ds(pl.multiple_of(i * 128, 128), 128)
        line = gain_ref[pl.ds(first_row + i, 1), :]
        column = jnp.broadcast_to(line, (128, 128)).T[:, 0:1]
        for ref in weights:
            ref[rows, :] = (ref[rows, :].astype(F32) * column).astype(BF16)
        return carry

    lax.fori_loop(0, count, step, 0)


def greet(me, senders, receivers_count, extra=None):
    barrier = pltpu.get_barrier_semaphore()
    for device in senders:
        pl.semaphore_signal(barrier, inc=1, device_id=device, device_id_type=MESH)
    if extra is not None:
        extra(barrier)
    pl.semaphore_wait(barrier, receivers_count)


def encoder_kernel(
    tokens_ref, history_ref, ids_ref, language_ref, gain_ref, gate_hbm, in_hbm, out_hbm,
    all_ref, memory_ref, quantized_ref, languages_ref,
    turned, base, blocks, w_gate, w_in, w_out, pre_send, relay_in, pre_in, pre_own,
    squares, squares_in, hidden, lang_send, code_pair, code_in, memory_all, lang_all,
    sums, theirs, first, both, up_z, down_z, up_tail, down_tail, tail_first, tail_both, result,
    send_sem, recv_sem, turn_sem, fan_send, fan_recv, load_sem,
):
    me = Place()
    x, y, z, c = me.x, me.y, me.z, me.c
    links = Links(send_sem, recv_sem)
    diagonal = x == y

    loads = [
        pltpu.make_async_copy(src, dst, load_sem.at[i])
        for i, (src, dst) in enumerate(((gate_hbm, w_gate), (in_hbm, w_in), (out_hbm, w_out)))
    ]
    for load in loads:
        load.start()

    def fan(barrier):
        for g in range(4):
            @pl.when(jnp.logical_not(jnp.logical_and(diagonal, x == g)))
            def _():
                pl.semaphore_signal(barrier, inc=1, device_id=me.at(y=x, x=g), device_id_type=MESH)

    turned[0] = tokens_ref[...].reshape(256, PART).T
    for e in range(4):
        turned[1, :, pl.ds(e * SEQ, SEQ)] = history_ref[ids_ref[e]].T
    lane = lax.broadcasted_iota(jnp.int32, (8, 128), 1)
    lines = jnp.zeros((8, 128), jnp.int32)
    for e in range(4):
        lines = jnp.where(lane == e, language_ref[e, 0], lines)
    lang_send[...] = lines

    greet(me, me.plane() + me.column(), jnp.where(diagonal, 11, 12), fan)

    other = me.at(y=x, x=y)
    turns = [
        pltpu.make_async_remote_copy(
            src_ref=turned.at[i], dst_ref=dst, send_sem=turn_sem.at[0, i], recv_sem=turn_sem.at[1, i],
            device_id=other, device_id_type=MESH)
        for i, dst in enumerate((blocks.at[y, z, c], base))
    ]

    @pl.when(jnp.logical_not(diagonal))
    def _():
        for turn in turns:
            turn.start()

    @pl.when(diagonal)
    def _():
        blocks[x, z, c] = turned[0]
        base[...] = turned[1]

    lang_copies = [links.start(lang_send, lang_all.at[y], me.at(y=me.yo(k))) for k in (1, 2, 3)]

    @pl.when(jnp.logical_not(diagonal))
    def _():
        turns[0].wait_recv()

    loads[0].wait()
    loads[1].wait()
    scale_rows((w_gate, w_in), gain_ref, y * 10, 10)
    gather_plane(links, me, blocks)

    ones = jnp.ones((8, 256), F32)

    def products(g):
        value = blocks[g].reshape(SLICE, 256)
        wide = value.astype(F32)
        squares[g] = ones * jnp.sum(wide * wide, axis=0, keepdims=True)
        return contract(w_gate[...], value), contract(w_in[...], value)

    up, down, far = me.yo(1), me.yo(-1), me.yo(2)
    to_up, to_down, to_far = me.at(y=up), me.at(y=down), me.at(y=far)
    gate, value = products(far)
    pre_send[far, 0] = gate.astype(BF16)
    relay_gate = links.start(pre_send.at[far, 0], relay_in.at[0], to_up)
    pre_send[far, 1] = value.astype(BF16)
    relay_value = links.start(pre_send.at[far, 1], relay_in.at[1], to_down)
    square_copies = [links.start(squares.at[far], squares_in.at[0], to_far)]
    gate, value = products(up)
    pre_send[up, 0] = gate.astype(BF16)
    pre_send[up, 1] = value.astype(BF16)
    straight_up = links.start(pre_send.at[up, 1], pre_in.at[0, 1], to_up)
    square_copies.append(links.start(squares.at[up], squares_in.at[1], to_up))
    gate, value = products(down)
    pre_send[down, 0] = gate.astype(BF16)
    straight_down = links.start(pre_send.at[down, 0], pre_in.at[1, 0], to_down)
    pre_send[down, 1] = value.astype(BF16)
    square_copies.append(links.start(squares.at[down], squares_in.at[2], to_down))
    relay_gate.wait_recv()
    add_to(pre_send.at[up, 0], relay_in.at[0])
    joint_up = links.start(pre_send.at[up, 0], pre_in.at[0, 0], to_up)
    relay_value.wait_recv()
    add_to(pre_send.at[down, 1], relay_in.at[1])
    joint_down = links.start(pre_send.at[down, 1], pre_in.at[1, 1], to_down)
    gate, value = products(y)
    pre_own[0] = gate
    pre_own[1] = value
    for copy in square_copies:
        copy.wait_recv()
    total = squares[y] + squares_in[0] + squares_in[1] + squares_in[2]
    inverse = lax.rsqrt(total * (1.0 / WIDTH) + EPS)[0:1, :]
    straight_up.wait_recv()
    straight_down.wait_recv()
    joint_up.wait_recv()
    joint_down.wait_recv()
    gate = (pre_own[0] + pre_in[0, 0].astype(F32) + pre_in[1, 0].astype(F32)) * inverse
    value = (pre_own[1] + pre_in[0, 1].astype(F32) + pre_in[1, 1].astype(F32)) * inverse
    hidden[y] = (gelu(gate) * value).astype(BF16)

    half = UNITS // 2
    out_up = links.start(hidden.at[y], hidden.at[y], to_up)
    out_down = links.start(hidden.at[y], hidden.at[y], to_down)
    loads[2].wait()
    partner = me.at(c=1 - c)
    core_copies = []

    def outward(g):
        sums[g] = contract(w_out[...], hidden[g]).astype(BF16).reshape(NZ, 2, PART, 256)
        core_copies.append((g, links.start(sums.at[g, :, 1 - c], theirs.at[g], partner)))

    outward(y)
    out_up.wait_recv()
    far_up = links.start(hidden.at[down, pl.ds(0, half)], hidden.at[down, pl.ds(0, half)], to_up)
    out_down.wait_recv()
    far_down = links.start(hidden.at[up, pl.ds(half, half)], hidden.at[up, pl.ds(half, half)], to_down)
    outward(down)
    outward(up)
    far_up.wait_recv()
    far_down.wait_recv()
    outward(far)

    scatter_plane(
        links, me,
        (sums, theirs, first, both, up_z, down_z, up_tail, down_tail, tail_first, tail_both, result),
        core_copies,
    )

    @pl.when(jnp.logical_not(diagonal))
    def _():
        turns[1].wait_recv()

    encoded = (blocks[x, z, c].astype(F32) + result[...]).astype(BF16)
    baseline = base[...].astype(F32)
    difference = encoded.astype(F32) - baseline
    example = lax.broadcasted_iota(jnp.int32, (PART, 256), 1) // SEQ
    size = jnp.abs(difference)
    scale = jnp.zeros((PART, 256), F32)
    for e in range(4):
        top = jnp.max(jnp.where(example == e, size, 0.0), axis=1, keepdims=True) + EPS
        scale = jnp.where(example == e, top, scale)
    codes = (difference / scale).astype(BF16)
    code_pair[0] = (baseline + codes.astype(F32) * scale).astype(BF16)
    code_pair[1] = codes

    fans = [
        pltpu.make_async_remote_copy(
            src_ref=code_pair.at[0], dst_ref=memory_all.at[x], send_sem=fan_send.at[l], recv_sem=fan_recv.at[x],
            device_id=me.at(y=l, x=y), device_id_type=MESH)
        for l in range(4)
    ]
    code_turn = pltpu.make_async_remote_copy(
        src_ref=code_pair.at[1], dst_ref=code_in, send_sem=turn_sem.at[0, 2], recv_sem=turn_sem.at[1, 2],
        device_id=other, device_id_type=MESH)
    arrivals = [
        pltpu.make_async_remote_copy(
            src_ref=code_pair.at[0], dst_ref=memory_all.at[g], send_sem=fan_send.at[g], recv_sem=fan_recv.at[g],
            device_id=other, device_id_type=MESH)
        for g in range(4)
    ]
    for l in range(4):
        @pl.when(jnp.logical_not(jnp.logical_and(diagonal, y == l)))
        def _():
            fans[l].start()

    @pl.when(jnp.logical_not(diagonal))
    def _():
        code_turn.start()

    @pl.when(diagonal)
    def _():
        memory_all[x] = code_pair[0]
        code_in[...] = code_pair[1]

    for copy in lang_copies:
        copy.wait_recv()
    lang_all[y] = lang_send[...]
    languages_ref[...] = lang_all[...]

    for g in range(4):
        @pl.when(jnp.logical_not(jnp.logical_and(diagonal, x == g)))
        def _():
            arrivals[g].wait_recv()

    @pl.when(jnp.logical_not(diagonal))
    def _():
        code_turn.wait_recv()

    all_ref[...] = memory_all[...]
    memory_ref[...] = memory_all[y].T.reshape(4, SEQ, PART)
    quantized_ref[...] = code_in[...].T.reshape(4, SEQ, PART)

    for l in range(4):
        @pl.when(jnp.logical_not(jnp.logical_and(diagonal, y == l)))
        def _():
            fans[l].wait_send()

    @pl.when(jnp.logical_not(diagonal))
    def _():
        code_turn.wait_send()
        for turn in turns:
            turn.wait_send()

    links.finish()


def decoder_kernel(
    rows, memory_ref, language_ref, gain_ref, gate_hbm, in_hbm, out_hbm,
    decoded_ref,
    blocks, own, w_gate, w_in, w_out, hidden, acc, finished,
    sums, theirs, first, both, up_z, down_z, up_tail, down_tail, tail_first, tail_both, result,
    send_sem, recv_sem, load_sem,
):
    me = Place()
    x, y, z, c = me.x, me.y, me.z, me.c
    links = Links(send_sem, recv_sem)
    loads = [
        pltpu.make_async_copy(src, dst, load_sem.at[i])
        for i, (src, dst) in enumerate(((gate_hbm, w_gate), (in_hbm, w_in), (out_hbm, w_out)))
    ]
    for load in loads:
        load.start()

    lane = lax.broadcasted_iota(jnp.int32, (SEQ, rows), 1)
    line = lax.broadcasted_iota(jnp.int32, (SEQ, rows), 0)
    count = jnp.int32(0)
    chosen = jnp.zeros((PART, rows), F32)
    for g in range(4):
        picks = []
        for e in range(4):
            mine = language_ref[g * 4 + e] == y
            start = jnp.where(mine, count * SEQ, -SEQ)
            count = count + mine.astype(jnp.int32)
            picks.append((lane == line + start).astype(F32).astype(BF16))
        chosen = chosen + jnp.dot(memory_ref[g], jnp.concatenate(picks, axis=0), preferred_element_type=F32)
    own[...] = chosen.astype(BF16)
    blocks[x, z, c] = own[...]

    greet(me, me.plane() + me.column(), 8)
    gather = functools.partial(gather_plane, links, me, blocks)
    loads[0].wait()
    loads[1].wait()
    scale_rows((w_gate, w_in), gain_ref, 0, 40)
    gather()

    total = jnp.zeros((1, rows), F32)
    for g in range(4):
        part = pl.ds(g * SLICE, SLICE)
        value = blocks[g].reshape(SLICE, rows)
        wide = value.astype(F32)
        total = total + jnp.sum(wide * wide, axis=0, keepdims=True)
        for i, w in enumerate((w_gate, w_in)):
            term = contract(w[part, :], value)
            acc[i] = term if g == 0 else acc[i] + term
    inverse = lax.rsqrt(total * (1.0 / WIDTH) + EPS)
    hidden[...] = (gelu(acc[0] * inverse) * (acc[1] * inverse)).astype(BF16)

    loads[2].wait()
    partner = me.at(c=1 - c)
    core_copies = []
    for g in range(4):
        product = contract(w_out[:, pl.ds(g * SLICE, SLICE)], hidden[...])
        sums[g] = product.astype(BF16).reshape(NZ, 2, PART, rows)
        core_copies.append((g, links.start(sums.at[g, :, 1 - c], theirs.at[g], partner)))
    scatter_plane(
        links, me,
        (sums, theirs, first, both, up_z, down_z, up_tail, down_tail, tail_first, tail_both, result),
        core_copies,
    )
    finished[y] = (own[...].astype(F32) + result[...]).astype(BF16)
    returns = [links.start(finished.at[y], finished.at[y], me.at(y=me.yo(k))) for k in (1, 2, 3)]

    place = lax.broadcasted_iota(jnp.int32, (rows, 256), 0)
    column = lax.broadcasted_iota(jnp.int32, (rows, 256), 1)
    example, token = column // SEQ, column % SEQ
    sources = []
    for l in range(4):
        source = jnp.full((rows, 256), -1, jnp.int32)
        for e in range(4):
            lang = language_ref[y * 4 + e]
            slot = jnp.int32(0)
            for other in range(16):
                ahead = jnp.logical_and(language_ref[other] == lang, other < y * 4 + e)
                slot = slot + ahead.astype(jnp.int32)
            start = jnp.where(lang == l, slot * SEQ, -SEQ)
            source = jnp.where(example == e, token + start, source)
        sources.append((place == source).astype(F32).astype(BF16))
    for copy in returns:
        copy.wait_recv()
    answer = jnp.zeros((PART, 256), F32)
    for l in range(4):
        answer = answer + jnp.dot(finished[l], sources[l], preferred_element_type=F32)
    decoded_ref[...] = answer.astype(BF16).T.reshape(4, SEQ, PART)
    links.finish()


VMEM = pl.BlockSpec(memory_space=pltpu.VMEM)
SMEM = pl.BlockSpec(memory_space=pltpu.SMEM)
ANY = pl.BlockSpec(memory_space=pl.ANY)
DMA = pltpu.SemaphoreType.DMA


def encode(tokens, history, ids, language, gain, gate, up, out):
    sds = jax.ShapeDtypeStruct
    return pl.pallas_call(
        encoder_kernel,
        out_shape=(
            sds((4, PART, 256), BF16),
            sds((4, SEQ, PART), BF16),
            sds((4, SEQ, PART), BF16),
            sds((4, 8, 128), jnp.int32),
        ),
        in_specs=[VMEM, VMEM, SMEM, SMEM, VMEM, ANY, ANY, ANY],
        out_specs=(VMEM, VMEM, VMEM, VMEM),
        scratch_shapes=[
            pltpu.VMEM((2, PART, 256), BF16),
            pltpu.VMEM((PART, 256), BF16),
            pltpu.VMEM((NX, NZ, 2, PART, 256), BF16),
            pltpu.VMEM((SLICE, UNITS), BF16),
            pltpu.VMEM((SLICE, UNITS), BF16),
            pltpu.VMEM((UNITS, SLICE), BF16),
            pltpu.VMEM((4, 2, UNITS, 256), BF16),
            pltpu.VMEM((2, UNITS, 256), BF16),
            pltpu.VMEM((2, 2, UNITS, 256), BF16),
            pltpu.VMEM((2, UNITS, 256), F32),
            pltpu.VMEM((4, 8, 256), F32),
            pltpu.VMEM((3, 8, 256), F32),
            pltpu.VMEM((4, UNITS, 256), BF16),
            pltpu.VMEM((8, 128), jnp.int32),
            pltpu.VMEM((2, PART, 256), BF16),
            pltpu.VMEM((PART, 256), BF16),
            pltpu.VMEM((4, PART, 256), BF16),
            pltpu.VMEM((4, 8, 128), jnp.int32),
            *scatter_shapes(256),
            DMA((COPIES + 32,)),
            DMA((COPIES + 32,)),
            DMA((2, 3)),
            DMA((4,)),
            DMA((4,)),
            DMA((3,)),
        ],
        compiler_params=pltpu.CompilerParams(
            collective_id=0, has_side_effects=True, vmem_limit_bytes=56 << 20
        ),
    )(tokens, history, ids, language, gain, gate, up, out)


def decode(rows, memory, language, gain, gate, up, out):
    return pl.pallas_call(
        functools.partial(decoder_kernel, rows),
        out_shape=jax.ShapeDtypeStruct((4, SEQ, PART), BF16),
        in_specs=[VMEM, SMEM, VMEM, ANY, ANY, ANY],
        out_specs=VMEM,
        scratch_shapes=[
            pltpu.VMEM((NX, NZ, 2, PART, rows), BF16),
            pltpu.VMEM((PART, rows), BF16),
            pltpu.VMEM((WIDTH, UNITS), BF16),
            pltpu.VMEM((WIDTH, UNITS), BF16),
            pltpu.VMEM((UNITS, WIDTH), BF16),
            pltpu.VMEM((UNITS, rows), BF16),
            pltpu.VMEM((2, UNITS, rows), F32),
            pltpu.VMEM((4, PART, rows), BF16),
            *scatter_shapes(rows),
            DMA((COPIES,)),
            DMA((COPIES,)),
            DMA((3,)),
        ],
        compiler_params=pltpu.CompilerParams(
            collective_id=1, has_side_effects=True, vmem_limit_bytes=56 << 20
        ),
    )(memory, language, gain, gate, up, out)


def shards(
    tokens, language, example_ids, history, enc_gain, dec_gain, enc_gate, enc_in, enc_out, dec_gate, dec_in, dec_out
):
    memory_all, new_memory, quantized, languages = encode(
        tokens, history, example_ids, language, enc_gain.reshape(40, 128), enc_gate, enc_in, enc_out
    )
    names = languages[:, 0, :4].reshape(16)
    decoded = decode(
        8 * SEQ, memory_all, names, dec_gain.reshape(40, 128), dec_gate[0], dec_in[0], dec_out[0]
    )
    return decoded, new_memory, quantized


def solution(mesh):
    in_specs = (
        P("section", None, "tp"),
        P("section", None),
        P("section"),
        P(None, None, "tp"),
        P(),
        P("section", None),
        P("section", "tp"),
        P("section", "tp"),
        P("tp", "section"),
        P("section", None, "tp"),
        P("section", None, "tp"),
        P("section", "tp", None),
    )
    out_specs = (P("section", None, "tp"), P("section", None, "tp"), P("section", None, "tp"))
    return jax.shard_map(shards, mesh=mesh, in_specs=in_specs, out_specs=out_specs, check_vma=False)
```

```python
import functools

import jax
import jax.numpy as jnp
from jax import lax
from jax.experimental import pallas as pl
from jax.experimental.pallas import tpu as pltpu
from jax.sharding import PartitionSpec as P

MESH = pl.DeviceIdType.MESH
BF16 = jnp.bfloat16
F32 = jnp.float32
EPS = 1e-06
NX, NZ, NY = 4, 8, 4
SEQ = 64
PART = 80
HEAD = 64
TAIL = PART - HEAD
SLICE = 1280
UNITS = 320
WIDTH = 5120
COPIES = 128


class Links:
    def __init__(self, send_sem, recv_sem):
        self.send_sem, self.recv_sem = send_sem, recv_sem
        self.count = 0
        self.sent = []

    def start(self, src, dst, device):
        copy = pltpu.make_async_remote_copy(
            src_ref=src,
            dst_ref=dst,
            send_sem=self.send_sem.at[self.count],
            recv_sem=self.recv_sem.at[self.count],
            device_id=device,
            device_id_type=MESH,
        )
        self.count += 1
        copy.start()
        self.sent.append(copy)
        return copy

    def finish(self):
        for copy in self.sent:
            copy.wait_send()
        self.sent = []


class Place:
    def __init__(self):
        self.y = lax.axis_index("section")
        t = lax.axis_index("tp")
        self.x, self.z, self.c = t // 16, (t // 2) % 8, t % 2
        self.d = 1 - 2 * self.c

    def at(self, y=None, x=None, z=None, c=None):
        y = self.y if y is None else y
        x = self.x if x is None else x
        z = self.z if z is None else z
        c = self.c if c is None else c
        return (y, (x * 8 + z) * 2 + c)

    def xo(self, off):
        return (self.x + off + 8) % 4

    def yo(self, off):
        return (self.y + off + 8) % 4

    def zo(self, off):
        return (self.z + off + 8) % 8

    def plane(self):
        others = [self.at(z=self.zo(off)) for off in NEAR]
        others += [self.at(x=self.xo(k)) for k in (1, 2, 3)]
        return others + [self.at(c=1 - self.c)]

    def column(self):
        return [self.at(y=self.yo(k)) for k in (1, 2, 3)]


NEAR = (1, 7, 2, 6, 3, 5, 4)
FAR = (4, 3, 5, 2, 6, 1, 7)


class TailAlong:
    def __init__(self, links, me, tails, landed):
        self.links, self.me, self.tails, self.landed = links, me, tails, landed
        self.copies = {}

    def send(self, off, source, step):
        ref = self.tails(self.me.zo(source))
        self.copies[off] = self.links.start(ref, ref, self.me.at(z=self.me.zo(step)))

    def begin(self):
        for off in (2, 6, 1, 7):
            self.send(off, 0, off)
        self.landed(self.tails(self.me.z))

    def arrive(self, off):
        self.copies[off].wait_recv()
        self.landed(self.tails(self.me.zo(-off)))

    def relay(self):
        self.arrive(2)
        self.send(3, -2, 1)
        self.arrive(6)
        self.send(5, 2, -1)
        self.send(4, 2 * self.me.d, -2 * self.me.d)

    def finish(self):
        for off in (1, 7, 3, 5, 4):
            self.arrive(off)


def gather_plane(links, me, blocks, meanwhile):
    x, z, c = me.x, me.z, me.c
    partner = me.at(c=1 - c)

    def head(xx, zz):
        return blocks.at[xx, zz, c, pl.ds(0, HEAD)]

    def tail(xx):
        return blocks.at[xx, z, c, pl.ds(HEAD, TAIL)]

    def heads(zz):
        return blocks.at[:, zz, c, pl.ds(0, HEAD)]

    def tails(zz):
        return blocks.at[:, zz, c, pl.ds(HEAD, TAIL)]

    def send(ref, device):
        return links.start(ref, ref, device)

    core = []

    def to_core(ref):
        core.append(send(ref, partner))

    tail_along = TailAlong(links, me, tails, to_core)
    tail_cross = [send(tail(x), me.at(x=me.xo(k))) for k in (1, 2, 3)]
    order = (0,) + NEAR
    cross, second = {}, {}

    def send_cross(off):
        block = head(x, me.zo(-off))
        cross[off] = [send(block, me.at(x=me.xo(k))) for k in (1, 3)]

    def hop(i):
        off = order[i]
        for copy in cross[off]:
            copy.wait_recv()
        k = 1 if i % 2 == 0 else -1
        second[off] = send(head(me.xo(-k), me.zo(-off)), me.at(x=me.xo(k)))

    def land(i):
        off = order[i]
        second[off].wait_recv()
        to_core(heads(me.zo(-off)))

    along = {off: send(head(x, z), me.at(z=me.zo(off))) for off in NEAR}
    send_cross(0)
    meanwhile()
    for i in range(1, 8):
        along[order[i]].wait_recv()
        send_cross(order[i])
        if i == 2:
            for copy in tail_cross:
                copy.wait_recv()
            tail_along.begin()
        if i >= 3:
            hop(i - 3)
        if i == 6:
            tail_along.relay()
    for i in range(5, 8):
        land(i - 5)
        hop(i)
    for i in range(3, 8):
        land(i)
    tail_along.finish()
    for copy in core:
        copy.wait_recv()


def gather_turned(links, me, blocks, own, column, fan_send, fan_recv, meanwhile):
    x, y, z, c = me.x, me.y, me.z, me.c
    partner = me.at(c=1 - c)
    diagonal = x == y

    def fan(stage, src, dst):
        copies = []
        for k in range(4):
            copies.append(pltpu.make_async_remote_copy(
                src_ref=src, dst_ref=dst, send_sem=fan_send.at[stage, k], recv_sem=fan_recv.at[stage, y],
                device_id=me.at(x=me.xo(k), y=x), device_id_type=MESH))

        @pl.when(jnp.logical_not(diagonal))
        def _():
            copies[0].start()

        @pl.when(diagonal)
        def _():
            dst[...] = src[...]

        for copy in copies[1:]:
            copy.start()
        arrivals = []
        for j in range(4):
            g = me.yo(j)
            arrivals.append(pltpu.make_async_remote_copy(
                src_ref=src, dst_ref=dst, send_sem=fan_send.at[stage, j], recv_sem=fan_recv.at[stage, g],
                device_id=me.at(x=me.xo(1), y=x), device_id_type=MESH))
        return copies, arrivals

    def land(fans):
        @pl.when(jnp.logical_not(diagonal))
        def _():
            fans[1][0].wait_recv()

        for copy in fans[1][1:]:
            copy.wait_recv()

    def send(src, dst, device):
        return links.start(src, dst, device)

    def heads(zz):
        return blocks.at[:, zz, c, pl.ds(0, HEAD)]

    def tails(zz):
        return blocks.at[:, zz, c, pl.ds(HEAD, TAIL)]

    first = own.at[pl.ds(0, HEAD)]
    tail_fan = fan(8, own.at[pl.ds(HEAD, TAIL)], blocks.at[y, z, c, pl.ds(HEAD, TAIL)])
    along = {off: send(first, column.at[z], me.at(z=me.zo(off))) for off in NEAR}
    fans = {0: fan(0, first, blocks.at[y, z, c, pl.ds(0, HEAD)])}
    meanwhile()
    core = []

    def to_core(ref):
        core.append(send(ref, ref, partner))

    tail_along = TailAlong(links, me, tails, to_core)
    for i, off in enumerate(NEAR):
        along[off].wait_recv()
        zz = me.zo(-off)
        fans[off] = fan(i + 1, column.at[zz], blocks.at[y, zz, c, pl.ds(0, HEAD)])
        if i == 1:
            land(tail_fan)
            tail_along.begin()
    for i, off in enumerate((0,) + NEAR):
        land(fans[off])
        to_core(heads(me.zo(-off)))
        if i == 2:
            tail_along.relay()
    tail_along.finish()
    for copy in core:
        copy.wait_recv()

    def finish():
        for copies, _ in [tail_fan] + [fans[off] for off in (0,) + NEAR]:
            @pl.when(jnp.logical_not(diagonal))
            def _():
                copies[0].wait_send()

            for copy in copies[1:]:
                copy.wait_send()

    return finish


def add_to(dst, *terms):
    total = dst[...].astype(F32)
    for term in terms:
        total = total + term[...].astype(F32)
    dst[...] = total.astype(dst.dtype)


def scatter_shapes(rows):
    return [
        pltpu.VMEM((NX, NZ, 2, PART, rows), BF16),
        pltpu.VMEM((NX, NZ, PART, rows), BF16),
        pltpu.VMEM((3, NZ, HEAD, rows), BF16),
        pltpu.VMEM((7, HEAD, rows), BF16),
        pltpu.VMEM((7, NX, TAIL, rows), BF16),
        pltpu.VMEM((3, TAIL, rows), BF16),
        pltpu.VMEM((PART, rows), F32),
    ]


def scatter_plane(links, me, bufs, parts):
    sums, theirs, cross_in, along_in, tail_along_in, tail_cross_in, result = bufs
    x, z, c = me.x, me.z, me.c

    def head(xx, zz):
        return sums.at[xx, zz, c, pl.ds(0, HEAD)]

    def tail(xx):
        return sums.at[xx, z, c, pl.ds(HEAD, TAIL)]

    def tails(zz):
        return sums.at[:, zz, c, pl.ds(HEAD, TAIL)]

    for xx, copy in parts:
        copy.wait_recv()
        add_to(sums.at[xx, :, c], theirs.at[xx])

    order = FAR + (0,)
    hops, direct, relayed, along, tail_along, tail_cross = {}, {}, {}, {}, {}, {}

    def tail_send(off, step):
        slot = len(tail_along)
        tail_along[slot] = links.start(tails(me.zo(off)), tail_along_in.at[slot], me.at(z=me.zo(step)))

    tail_send(3, 1)
    tail_send(5, -1)
    tail_send(4, 2 * me.d)
    for i, off in enumerate(order):
        k = 1 if i % 2 == 0 else -1
        hops[i] = links.start(head(me.xo(2), me.zo(off)), cross_in.at[0, off], me.at(x=me.xo(k)))
        direct[i] = links.start(head(me.xo(-k), me.zo(off)), cross_in.at[1, off], me.at(x=me.xo(-k)))

    def relay(i):
        off = order[i]
        k = 1 if i % 2 == 0 else -1
        hops[i].wait_recv()
        add_to(head(me.xo(k), me.zo(off)), cross_in.at[0, off])
        relayed[i] = links.start(head(me.xo(k), me.zo(off)), cross_in.at[2, off], me.at(x=me.xo(k)))

    def collect(i):
        off = order[i]
        direct[i].wait_recv()
        relayed[i].wait_recv()
        add_to(head(x, me.zo(off)), cross_in.at[1, off], cross_in.at[2, off])
        if off:
            along[off] = links.start(head(x, me.zo(off)), along_in.at[off - 1], me.at(z=me.zo(off)))

    for i in range(8):
        relay(i)
        if i == 3:
            for copy in list(tail_along.values()):
                copy.wait_recv()
            add_to(tails(me.zo(2)), tail_along_in.at[0])
            add_to(tails(me.zo(-2)), tail_along_in.at[1])
            add_to(tails(me.zo(2 * me.d)), tail_along_in.at[2])
            for step in (2, -2, 1, -1):
                tail_send(step, step)
        if i >= 4:
            collect(i - 4)
    for slot in range(3, 7):
        tail_along[slot].wait_recv()
    add_to(tails(z), *[tail_along_in.at[i] for i in range(3, 7)])
    for k in (2, 1, 3):
        tail_cross[k] = links.start(tail(me.xo(k)), tail_cross_in.at[k - 1], me.at(x=me.xo(k)))
    for i in range(4, 8):
        collect(i)
    for off in FAR:
        along[off].wait_recv()
    total = head(x, z)[...].astype(F32)
    for i in range(7):
        total = total + along_in[i].astype(F32)
    result[pl.ds(0, HEAD)] = total
    for k in (2, 1, 3):
        tail_cross[k].wait_recv()
    total = tail(x)[...].astype(F32)
    for i in range(3):
        total = total + tail_cross_in[i].astype(F32)
    result[pl.ds(HEAD, TAIL)] = total


def first_weights(w_first, gate_hbm, in_hbm):
    return [(gate_hbm, w_first.at[pl.ds(0, UNITS)]), (in_hbm, w_first.at[pl.ds(UNITS, UNITS)])]


def contract(a, b):
    return lax.dot_general(a, b, (((0,), (0,)), ((), ())), preferred_element_type=F32)


def gelu(v):
    return jax.nn.gelu(v)


def scale_columns(weights, gain_ref, first_row, count):
    def step(i, carry):
        columns = pl.ds(pl.multiple_of(i * 128, 128), 128)
        line = gain_ref[pl.ds(first_row + i, 1), :]
        weights[:, columns] = (weights[:, columns].astype(F32) * line).astype(BF16)
        return carry

    lax.fori_loop(0, count, step, 0)


def greet(me, senders, receivers_count, extra=None):
    barrier = pltpu.get_barrier_semaphore()
    for device in senders:
        pl.semaphore_signal(barrier, inc=1, device_id=device, device_id_type=MESH)
    if extra is not None:
        extra(barrier)
    pl.semaphore_wait(barrier, receivers_count)


def encoder_kernel(
    tokens_ref, history_ref, ids_ref, language_ref, gain_ref, gate_hbm, in_hbm, out_hbm,
    all_ref, memory_ref, quantized_ref, languages_ref, branch_ref,
    turned, column, base, blocks, w_first, w_out, pre_send, relay_in, pre_in, pre_own,
    squares, squares_in, squares_core, hidden, lang_send, code_pair, code_in, memory_all, lang_all,
    sums, theirs, cross_in, along_in, tail_along_in, tail_cross_in, result,
    send_sem, recv_sem, turn_sem, wide_send, wide_recv, fan_send, fan_recv, load_sem,
):
    me = Place()
    x, y, z, c = me.x, me.y, me.z, me.c
    links = Links(send_sem, recv_sem)
    diagonal = x == y

    loads = [
        pltpu.make_async_copy(src, dst, load_sem.at[i])
        for i, (src, dst) in enumerate(first_weights(w_first, gate_hbm, in_hbm) + [(out_hbm, w_out)])
    ]
    for load in loads:
        load.start()

    def fan(barrier):
        for k in range(4):
            for device in (me.at(x=y, y=me.yo(k)), me.at(x=me.xo(k), y=x)):
                if k:
                    pl.semaphore_signal(barrier, inc=1, device_id=device, device_id_type=MESH)
                else:
                    @pl.when(jnp.logical_not(diagonal))
                    def _():
                        pl.semaphore_signal(barrier, inc=1, device_id=device, device_id_type=MESH)

    turned[0] = tokens_ref[...].reshape(256, PART).T
    for e in range(4):
        turned[1, :, pl.ds(e * SEQ, SEQ)] = history_ref[ids_ref[e]].T
    lane = lax.broadcasted_iota(jnp.int32, (8, 128), 1)
    lines = jnp.zeros((8, 128), jnp.int32)
    for e in range(4):
        lines = jnp.where(lane == e, language_ref[e], lines)
    lang_send[...] = lines

    greet(me, me.plane() + me.column(), jnp.where(diagonal, 20, 22), fan)

    other = me.at(y=x, x=y)
    turn = pltpu.make_async_remote_copy(
        src_ref=turned.at[1], dst_ref=base, send_sem=turn_sem.at[0, 0], recv_sem=turn_sem.at[1, 0],
        device_id=other, device_id_type=MESH)

    def meanwhile():
        @pl.when(jnp.logical_not(diagonal))
        def _():
            turn.start()

        @pl.when(diagonal)
        def _():
            base[...] = turned[1]

        loads[0].wait()
        loads[1].wait()
        scale_columns(w_first, gain_ref, y * 10, 10)

    lang_copies = [links.start(lang_send, lang_all.at[y], me.at(y=me.yo(k))) for k in (1, 2, 3)]

    finish_gather = gather_turned(
        links, me, blocks, turned.at[0], column, wide_send, wide_recv, meanwhile)

    ones = jnp.ones((8, 256), F32)

    def products(g):
        wide = blocks[g, :, c].astype(F32).reshape(SLICE // 2, 256)
        squares[g] = ones * jnp.sum(wide * wide, axis=0, keepdims=True)
        product = jnp.dot(w_first[...], blocks[g].reshape(SLICE, 256), preferred_element_type=F32)
        return product[:UNITS], product[UNITS:]

    up, down, far = me.yo(1), me.yo(-1), me.yo(2)
    to_up, to_down, to_far = me.at(y=up), me.at(y=down), me.at(y=far)
    gate, value = products(far)
    pre_send[far, 0] = gate.astype(BF16)
    relay_gate = links.start(pre_send.at[far, 0], relay_in.at[0], to_up)
    pre_send[far, 1] = value.astype(BF16)
    relay_value = links.start(pre_send.at[far, 1], relay_in.at[1], to_down)
    square_copies = [links.start(squares.at[far], squares_in.at[0], to_far)]
    gate, value = products(up)
    pre_send[up, 0] = gate.astype(BF16)
    pre_send[up, 1] = value.astype(BF16)
    straight_up = links.start(pre_send.at[up, 1], pre_in.at[0, 1], to_up)
    square_copies.append(links.start(squares.at[up], squares_in.at[1], to_up))
    gate, value = products(down)
    pre_send[down, 0] = gate.astype(BF16)
    straight_down = links.start(pre_send.at[down, 0], pre_in.at[1, 0], to_down)
    pre_send[down, 1] = value.astype(BF16)
    square_copies.append(links.start(squares.at[down], squares_in.at[2], to_down))
    relay_gate.wait_recv()
    add_to(pre_send.at[up, 0], relay_in.at[0])
    joint_up = links.start(pre_send.at[up, 0], pre_in.at[0, 0], to_up)
    relay_value.wait_recv()
    add_to(pre_send.at[down, 1], relay_in.at[1])
    joint_down = links.start(pre_send.at[down, 1], pre_in.at[1, 1], to_down)
    gate, value = products(y)
    pre_own[0] = gate
    pre_own[1] = value
    for copy in square_copies:
        copy.wait_recv()
    squares_core[0] = squares[y] + squares_in[0] + squares_in[1] + squares_in[2]
    core_square = links.start(squares_core.at[0], squares_core.at[1], me.at(c=1 - c))
    core_square.wait_recv()
    total = squares_core[0] + squares_core[1]
    inverse = lax.rsqrt(total * (1.0 / WIDTH) + EPS)[0:1, :]
    straight_up.wait_recv()
    straight_down.wait_recv()
    joint_up.wait_recv()
    joint_down.wait_recv()
    gate = (pre_own[0] + pre_in[0, 0].astype(F32) + pre_in[1, 0].astype(F32)) * inverse
    value = (pre_own[1] + pre_in[0, 1].astype(F32) + pre_in[1, 1].astype(F32)) * inverse
    hidden[y] = (gelu(gate) * value).astype(BF16)

    half = UNITS // 2
    out_up = links.start(hidden.at[y], hidden.at[y], to_up)
    out_down = links.start(hidden.at[y], hidden.at[y], to_down)
    loads[2].wait()
    partner = me.at(c=1 - c)
    core_copies = []

    def outward(g):
        sums[g] = contract(w_out[...], hidden[g]).astype(BF16).reshape(NZ, 2, PART, 256)
        core_copies.append((g, links.start(sums.at[g, :, 1 - c], theirs.at[g], partner)))

    outward(y)
    out_up.wait_recv()
    far_up = links.start(hidden.at[down, pl.ds(0, half)], hidden.at[down, pl.ds(0, half)], to_up)
    out_down.wait_recv()
    far_down = links.start(hidden.at[up, pl.ds(half, half)], hidden.at[up, pl.ds(half, half)], to_down)
    outward(down)
    outward(up)
    far_up.wait_recv()
    far_down.wait_recv()
    outward(far)

    scatter_plane(
        links, me,
        (sums, theirs, cross_in, along_in, tail_along_in, tail_cross_in, result),
        core_copies,
    )

    @pl.when(jnp.logical_not(diagonal))
    def _():
        turn.wait_recv()

    encoded = (blocks[x, z, c].astype(F32) + result[...]).astype(BF16)
    baseline = base[...].astype(F32)
    difference = encoded.astype(F32) - baseline
    example = lax.broadcasted_iota(jnp.int32, (PART, 256), 1) // SEQ
    size = jnp.abs(difference)
    scale = jnp.zeros((PART, 256), F32)
    for e in range(4):
        top = jnp.max(jnp.where(example == e, size, 0.0), axis=1, keepdims=True) + EPS
        scale = jnp.where(example == e, top, scale)
    codes = (difference / scale).astype(BF16)
    code_pair[0] = (baseline + codes.astype(F32) * scale).astype(BF16)
    code_pair[1] = codes

    fans = [
        pltpu.make_async_remote_copy(
            src_ref=code_pair.at[0], dst_ref=memory_all.at[x], send_sem=fan_send.at[l], recv_sem=fan_recv.at[x],
            device_id=me.at(y=l, x=y), device_id_type=MESH)
        for l in range(4)
    ]
    code_turn = pltpu.make_async_remote_copy(
        src_ref=code_pair.at[1], dst_ref=code_in, send_sem=turn_sem.at[0, 1], recv_sem=turn_sem.at[1, 1],
        device_id=other, device_id_type=MESH)
    arrivals = [
        pltpu.make_async_remote_copy(
            src_ref=code_pair.at[0], dst_ref=memory_all.at[g], send_sem=fan_send.at[g], recv_sem=fan_recv.at[g],
            device_id=other, device_id_type=MESH)
        for g in range(4)
    ]
    for l in range(4):
        @pl.when(jnp.logical_not(jnp.logical_and(diagonal, y == l)))
        def _():
            fans[l].start()

    @pl.when(jnp.logical_not(diagonal))
    def _():
        code_turn.start()

    @pl.when(diagonal)
    def _():
        memory_all[x] = code_pair[0]
        code_in[...] = code_pair[1]

    for copy in lang_copies:
        copy.wait_recv()
    lang_all[y] = lang_send[...]
    languages_ref[...] = lang_all[...]
    named = jnp.where(lane < 4, lang_all[...].astype(F32), -1.0)[:, 0:1]
    most = jnp.float32(0)
    for l in range(4):
        most = jnp.maximum(most, jnp.sum((named == l).astype(F32)))
    branch_ref[0] = (most > 4).astype(jnp.int32) + (most > 6).astype(jnp.int32)

    for g in range(4):
        @pl.when(jnp.logical_not(jnp.logical_and(diagonal, x == g)))
        def _():
            arrivals[g].wait_recv()

    @pl.when(jnp.logical_not(diagonal))
    def _():
        code_turn.wait_recv()

    all_ref[...] = memory_all[...]
    memory_ref[...] = memory_all[y].T.reshape(4, SEQ, PART)
    quantized_ref[...] = code_in[...].T.reshape(4, SEQ, PART)

    for l in range(4):
        @pl.when(jnp.logical_not(jnp.logical_and(diagonal, y == l)))
        def _():
            fans[l].wait_send()

    @pl.when(jnp.logical_not(diagonal))
    def _():
        code_turn.wait_send()
        turn.wait_send()

    finish_gather()

    links.finish()


def decoder_kernel(
    rows, memory_ref, language_ref, gain_ref, gate_hbm, in_hbm, out_hbm,
    decoded_ref,
    blocks, own, w_first, w_out, hidden, acc, squares, finished,
    sums, theirs, cross_in, along_in, tail_along_in, tail_cross_in, result,
    send_sem, recv_sem, load_sem,
):
    me = Place()
    x, y, z, c = me.x, me.y, me.z, me.c
    links = Links(send_sem, recv_sem)
    loads = [
        pltpu.make_async_copy(src, dst, load_sem.at[i])
        for i, (src, dst) in enumerate(first_weights(w_first, gate_hbm, in_hbm) + [(out_hbm, w_out)])
    ]
    for load in loads:
        load.start()

    lane = lax.broadcasted_iota(jnp.int32, (SEQ, rows), 1)
    line = lax.broadcasted_iota(jnp.int32, (SEQ, rows), 0)
    count = jnp.int32(0)
    chosen = jnp.zeros((PART, rows), F32)
    for g in range(4):
        picks = []
        for e in range(4):
            mine = language_ref[g, 0, e] == y
            start = jnp.where(mine, count * SEQ, -SEQ)
            count = count + mine.astype(jnp.int32)
            picks.append((lane == line + start).astype(F32).astype(BF16))
        chosen = chosen + jnp.dot(memory_ref[g], jnp.concatenate(picks, axis=0), preferred_element_type=F32)
    own[...] = chosen.astype(BF16)
    blocks[x, z, c] = own[...]

    greet(me, me.plane() + me.column(), 14)

    def meanwhile():
        loads[0].wait()
        loads[1].wait()
        scale_columns(w_first, gain_ref, 0, 40)

    gather_plane(links, me, blocks, meanwhile)

    total = jnp.zeros((1, rows), F32)
    for g in range(4):
        wide = blocks[g, :, c].astype(F32).reshape(SLICE // 2, rows)
        total = total + jnp.sum(wide * wide, axis=0, keepdims=True)
    partner = me.at(c=1 - c)
    squares[0] = jnp.broadcast_to(total, (8, rows))
    core_square = links.start(squares.at[0], squares.at[1], partner)
    for g in range(4):
        part = pl.ds(g * SLICE, SLICE)
        term = jnp.dot(w_first[:, part], blocks[g].reshape(SLICE, rows), preferred_element_type=F32)
        acc[...] = term if g == 0 else acc[...] + term
    core_square.wait_recv()
    inverse = lax.rsqrt((squares[0] + squares[1]) * (1.0 / WIDTH) + EPS)[0:1, :]
    hidden[...] = (gelu(acc[:UNITS] * inverse) * (acc[UNITS:] * inverse)).astype(BF16)

    loads[2].wait()
    core_copies = []
    for k in (2, 1, 3, 0):
        g = me.xo(k)
        columns = pl.ds(pl.multiple_of(g * SLICE, 128), SLICE)
        product = contract(w_out[:, columns], hidden[...])
        sums[g] = product.astype(BF16).reshape(NZ, 2, PART, rows)
        core_copies.append((g, links.start(sums.at[g, :, 1 - c], theirs.at[g], partner)))
    scatter_plane(
        links, me,
        (sums, theirs, cross_in, along_in, tail_along_in, tail_cross_in, result),
        core_copies,
    )
    finished[y] = (own[...].astype(F32) + result[...]).astype(BF16)
    returns = [links.start(finished.at[y], finished.at[y], me.at(y=me.yo(k))) for k in (1, 2, 3)]

    place = lax.broadcasted_iota(jnp.int32, (rows, 256), 0)
    column = lax.broadcasted_iota(jnp.int32, (rows, 256), 1)
    example, token = column // SEQ, column % SEQ
    sources = []
    for l in range(4):
        source = jnp.full((rows, 256), -1, jnp.int32)
        for e in range(4):
            lang = language_ref[y, 0, e]
            slot = jnp.int32(0)
            for other in range(16):
                ahead = jnp.logical_and(language_ref[other // 4, 0, other % 4] == lang, other < y * 4 + e)
                slot = slot + ahead.astype(jnp.int32)
            start = jnp.where(lang == l, slot * SEQ, -SEQ)
            source = jnp.where(example == e, token + start, source)
        sources.append((place == source).astype(F32).astype(BF16))
    for copy in returns:
        copy.wait_recv()
    answer = jnp.zeros((PART, 256), F32)
    for l in range(4):
        answer = answer + jnp.dot(finished[l], sources[l], preferred_element_type=F32)
    decoded_ref[...] = answer.astype(BF16).T.reshape(4, SEQ, PART)
    links.finish()


VMEM = pl.BlockSpec(memory_space=pltpu.VMEM)
SMEM = pl.BlockSpec(memory_space=pltpu.SMEM)
ANY = pl.BlockSpec(memory_space=pl.ANY)
DMA = pltpu.SemaphoreType.DMA


def encode(tokens, history, ids, language, gain, gate, up, out):
    sds = jax.ShapeDtypeStruct
    return pl.pallas_call(
        encoder_kernel,
        out_shape=(
            sds((4, PART, 256), BF16),
            sds((4, SEQ, PART), BF16),
            sds((4, SEQ, PART), BF16),
            sds((4, 8, 128), jnp.int32),
            sds((1,), jnp.int32),
        ),
        in_specs=[VMEM, VMEM, SMEM, SMEM, VMEM, ANY, ANY, ANY],
        out_specs=(VMEM, VMEM, VMEM, VMEM, SMEM),
        scratch_shapes=[
            pltpu.VMEM((2, PART, 256), BF16),
            pltpu.VMEM((NZ, HEAD, 256), BF16),
            pltpu.VMEM((PART, 256), BF16),
            pltpu.VMEM((NX, NZ, 2, PART, 256), BF16),
            pltpu.VMEM((2 * UNITS, SLICE), BF16),
            pltpu.VMEM((UNITS, SLICE), BF16),
            pltpu.VMEM((4, 2, UNITS, 256), BF16),
            pltpu.VMEM((2, UNITS, 256), BF16),
            pltpu.VMEM((2, 2, UNITS, 256), BF16),
            pltpu.VMEM((2, UNITS, 256), F32),
            pltpu.VMEM((4, 8, 256), F32),
            pltpu.VMEM((3, 8, 256), F32),
            pltpu.VMEM((2, 8, 256), F32),
            pltpu.VMEM((4, UNITS, 256), BF16),
            pltpu.VMEM((8, 128), jnp.int32),
            pltpu.VMEM((2, PART, 256), BF16),
            pltpu.VMEM((PART, 256), BF16),
            pltpu.VMEM((4, PART, 256), BF16),
            pltpu.VMEM((4, 8, 128), jnp.int32),
            *scatter_shapes(256),
            DMA((COPIES,)),
            DMA((COPIES,)),
            DMA((2, 2)),
            DMA((9, 4)),
            DMA((9, 4)),
            DMA((4,)),
            DMA((4,)),
            DMA((3,)),
        ],
        compiler_params=pltpu.CompilerParams(
            collective_id=0, has_side_effects=True, vmem_limit_bytes=56 << 20
        ),
    )(tokens, history, ids, language, gain, gate, up, out)


def decode(rows, number, memory, language, gain, gate, up, out):
    return pl.pallas_call(
        functools.partial(decoder_kernel, rows),
        out_shape=jax.ShapeDtypeStruct((4, SEQ, PART), BF16),
        in_specs=[VMEM, SMEM, VMEM, ANY, ANY, ANY],
        out_specs=VMEM,
        scratch_shapes=[
            pltpu.VMEM((NX, NZ, 2, PART, rows), BF16),
            pltpu.VMEM((PART, rows), BF16),
            pltpu.VMEM((2 * UNITS, WIDTH), BF16),
            pltpu.VMEM((UNITS, WIDTH), BF16),
            pltpu.VMEM((UNITS, rows), BF16),
            pltpu.VMEM((2 * UNITS, rows), F32),
            pltpu.VMEM((2, 8, rows), F32),
            pltpu.VMEM((4, PART, rows), BF16),
            *scatter_shapes(rows),
            DMA((COPIES,)),
            DMA((COPIES,)),
            DMA((3,)),
        ],
        compiler_params=pltpu.CompilerParams(
            collective_id=number, has_side_effects=True, vmem_limit_bytes=56 << 20
        ),
    )(memory, language, gain, gate, up, out)


def shards(
    tokens, language, example_ids, history, enc_gain, dec_gain, enc_gate, enc_in, enc_out, dec_gate, dec_in, dec_out
):
    memory_all, new_memory, quantized, languages, branch = encode(
        tokens, history, example_ids, language.reshape(4), enc_gain.reshape(40, 128), enc_gate.T, enc_in.T, enc_out
    )
    decoded = lax.switch(
        branch[0],
        [functools.partial(decode, rows * SEQ, number) for number, rows in ((1, 4), (2, 6), (3, 8))],
        memory_all, languages, dec_gain.reshape(40, 128), dec_gate[0].T, dec_in[0].T, dec_out[0],
    )
    return decoded, new_memory, quantized


def solution(mesh):
    in_specs = (
        P("section", None, "tp"),
        P("section", None),
        P("section"),
        P(None, None, "tp"),
        P(),
        P("section", None),
        P("section", "tp"),
        P("section", "tp"),
        P("tp", "section"),
        P("section", None, "tp"),
        P("section", None, "tp"),
        P("section", "tp", None),
    )
    out_specs = (P("section", None, "tp"), P("section", None, "tp"), P("section", None, "tp"))
    return jax.shard_map(shards, mesh=mesh, in_specs=in_specs, out_specs=out_specs, check_vma=False)
```

```python
import functools

import jax
import jax.numpy as jnp
from jax import lax
from jax.experimental import pallas as pl
from jax.experimental.pallas import tpu as pltpu
from jax.sharding import PartitionSpec as P

MESH = pl.DeviceIdType.MESH
BF16 = jnp.bfloat16
F32 = jnp.float32
EPS = 1e-06
NX, NZ, NY = 4, 8, 4
SEQ = 64
PART = 80
HEAD = 64
TAIL = PART - HEAD
SLICE = 1280
UNITS = 320
WIDTH = 5120
COPIES = 128
PAIR = 2 * SEQ


class Links:
    def __init__(self, send_sem, recv_sem):
        self.send_sem, self.recv_sem = send_sem, recv_sem
        self.count = 0
        self.sent = []

    def start(self, src, dst, device):
        copy = pltpu.make_async_remote_copy(
            src_ref=src,
            dst_ref=dst,
            send_sem=self.send_sem.at[self.count],
            recv_sem=self.recv_sem.at[self.count],
            device_id=device,
            device_id_type=MESH,
        )
        self.count += 1
        copy.start()
        self.sent.append(copy)
        return copy

    def finish(self):
        for copy in self.sent:
            copy.wait_send()
        self.sent = []


class Place:
    def __init__(self):
        self.y = lax.axis_index("section")
        t = lax.axis_index("tp")
        self.x, self.z, self.c = t // 16, (t // 2) % 8, t % 2
        self.d = 1 - 2 * self.c

    def at(self, y=None, x=None, z=None, c=None):
        y = self.y if y is None else y
        x = self.x if x is None else x
        z = self.z if z is None else z
        c = self.c if c is None else c
        return (y, (x * 8 + z) * 2 + c)

    def xo(self, off):
        return (self.x + off + 8) % 4

    def yo(self, off):
        return (self.y + off + 8) % 4

    def zo(self, off):
        return (self.z + off + 8) % 8

    def plane(self):
        others = [self.at(z=self.zo(off)) for off in NEAR]
        others += [self.at(x=self.xo(k)) for k in (1, 2, 3)]
        return others + [self.at(c=1 - self.c)]

    def column(self):
        return [self.at(y=self.yo(k)) for k in (1, 2, 3)]


NEAR = (1, 7, 2, 6, 3, 5, 4)
FAR = (4, 3, 5, 2, 6, 1, 7)


class TailAlong:
    def __init__(self, links, me, tails, landed):
        self.links, self.me, self.tails, self.landed = links, me, tails, landed
        self.copies = {}

    def send(self, off, source, step):
        ref = self.tails(self.me.zo(source))
        self.copies[off] = self.links.start(ref, ref, self.me.at(z=self.me.zo(step)))

    def begin(self):
        for off in (2, 6, 1, 7):
            self.send(off, 0, off)
        self.landed(self.tails(self.me.z))

    def arrive(self, off):
        self.copies[off].wait_recv()
        self.landed(self.tails(self.me.zo(-off)))

    def relay(self):
        self.arrive(2)
        self.send(3, -2, 1)
        self.arrive(6)
        self.send(5, 2, -1)
        self.send(4, 2 * self.me.d, -2 * self.me.d)

    def finish(self):
        for off in (1, 7, 3, 5, 4):
            self.arrive(off)


def gather_plane(links, me, blocks, meanwhile, seen):
    x, z, c = me.x, me.z, me.c
    partner = me.at(c=1 - c)

    def head(xx, zz):
        return blocks.at[xx, zz, c, pl.ds(0, HEAD)]

    def tail(xx):
        return blocks.at[xx, z, c, pl.ds(HEAD, TAIL)]

    def heads(zz):
        return blocks.at[:, zz, c, pl.ds(0, HEAD)]

    def tails(zz):
        return blocks.at[:, zz, c, pl.ds(HEAD, TAIL)]

    def send(ref, device):
        return links.start(ref, ref, device)

    core = []

    def to_core(ref):
        core.append(send(ref, partner))
        seen(ref)

    tail_along = TailAlong(links, me, tails, to_core)
    tail_cross = [send(tail(x), me.at(x=me.xo(k))) for k in (1, 2, 3)]
    order = (0,) + NEAR
    cross, second = {}, {}

    def send_cross(off):
        block = head(x, me.zo(-off))
        cross[off] = [send(block, me.at(x=me.xo(k))) for k in (1, 3)]

    def hop(i):
        off = order[i]
        for copy in cross[off]:
            copy.wait_recv()
        k = 1 if i % 2 == 0 else -1
        second[off] = send(head(me.xo(-k), me.zo(-off)), me.at(x=me.xo(k)))

    def land(i):
        off = order[i]
        second[off].wait_recv()
        to_core(heads(me.zo(-off)))

    along = {off: send(head(x, z), me.at(z=me.zo(off))) for off in NEAR}
    send_cross(0)
    for i in range(1, 8):
        meanwhile(i - 1)
        along[order[i]].wait_recv()
        send_cross(order[i])
        if i == 2:
            for copy in tail_cross:
                copy.wait_recv()
            tail_along.begin()
        if i >= 3:
            hop(i - 3)
        if i == 6:
            tail_along.relay()
    meanwhile(7)
    for i in range(5, 8):
        land(i - 5)
        hop(i)
    for i in range(3, 8):
        land(i)
    tail_along.finish()
    for copy in core:
        copy.wait_recv()


def gather_turned(links, me, blocks, own, column, fan_send, fan_recv, meanwhile):
    x, y, z, c = me.x, me.y, me.z, me.c
    partner = me.at(c=1 - c)
    diagonal = x == y

    def fan(stage, src, dst):
        copies = []
        for k in range(4):
            copies.append(pltpu.make_async_remote_copy(
                src_ref=src, dst_ref=dst, send_sem=fan_send.at[stage, k], recv_sem=fan_recv.at[stage, y],
                device_id=me.at(x=me.xo(k), y=x), device_id_type=MESH))

        @pl.when(jnp.logical_not(diagonal))
        def _():
            copies[0].start()

        @pl.when(diagonal)
        def _():
            dst[...] = src[...]

        for copy in copies[1:]:
            copy.start()
        arrivals = []
        for j in range(4):
            g = me.yo(j)
            arrivals.append(pltpu.make_async_remote_copy(
                src_ref=src, dst_ref=dst, send_sem=fan_send.at[stage, j], recv_sem=fan_recv.at[stage, g],
                device_id=me.at(x=me.xo(1), y=x), device_id_type=MESH))
        return copies, arrivals

    def land(fans):
        @pl.when(jnp.logical_not(diagonal))
        def _():
            fans[1][0].wait_recv()

        for copy in fans[1][1:]:
            copy.wait_recv()

    def send(src, dst, device):
        return links.start(src, dst, device)

    def heads(zz):
        return blocks.at[:, zz, c, pl.ds(0, HEAD)]

    def tails(zz):
        return blocks.at[:, zz, c, pl.ds(HEAD, TAIL)]

    first = own.at[pl.ds(0, HEAD)]
    tail_fan = fan(8, own.at[pl.ds(HEAD, TAIL)], blocks.at[y, z, c, pl.ds(HEAD, TAIL)])
    along = {off: send(first, column.at[z], me.at(z=me.zo(off))) for off in NEAR}
    fans = {0: fan(0, first, blocks.at[y, z, c, pl.ds(0, HEAD)])}
    meanwhile()
    core = []

    def to_core(ref):
        core.append(send(ref, ref, partner))

    tail_along = TailAlong(links, me, tails, to_core)
    for i, off in enumerate(NEAR):
        along[off].wait_recv()
        zz = me.zo(-off)
        fans[off] = fan(i + 1, column.at[zz], blocks.at[y, zz, c, pl.ds(0, HEAD)])
        if i == 1:
            land(tail_fan)
            tail_along.begin()
    for i, off in enumerate((0,) + NEAR):
        land(fans[off])
        to_core(heads(me.zo(-off)))
        if i == 2:
            tail_along.relay()
    tail_along.finish()
    for copy in core:
        copy.wait_recv()

    def finish():
        for copies, _ in [tail_fan] + [fans[off] for off in (0,) + NEAR]:
            @pl.when(jnp.logical_not(diagonal))
            def _():
                copies[0].wait_send()

            for copy in copies[1:]:
                copy.wait_send()

    return finish


def add_to(dst, *terms):
    total = dst[...].astype(F32)
    for term in terms:
        total = total + term[...].astype(F32)
    dst[...] = total.astype(dst.dtype)


def scatter_shapes(rows):
    return [
        pltpu.VMEM((NX, NZ, 2, PART, rows), BF16),
        pltpu.VMEM((NX, NZ, PART, rows), BF16),
        pltpu.VMEM((3, NZ, HEAD, rows), BF16),
        pltpu.VMEM((7, HEAD, rows), BF16),
        pltpu.VMEM((7, NX, TAIL, rows), BF16),
        pltpu.VMEM((3, TAIL, rows), BF16),
        pltpu.VMEM((PART, rows), F32),
    ]


def scatter_plane(links, me, bufs, parts):
    sums, theirs, cross_in, along_in, tail_along_in, tail_cross_in, result = bufs
    x, z, c = me.x, me.z, me.c

    def head(xx, zz):
        return sums.at[xx, zz, c, pl.ds(0, HEAD)]

    def tail(xx):
        return sums.at[xx, z, c, pl.ds(HEAD, TAIL)]

    def tails(zz):
        return sums.at[:, zz, c, pl.ds(HEAD, TAIL)]

    for xx, copy in parts:
        copy.wait_recv()
        add_to(sums.at[xx, :, c], theirs.at[xx])

    order = FAR + (0,)
    hops, direct, relayed, along, tail_along, tail_cross = {}, {}, {}, {}, {}, {}

    def tail_send(off, step):
        slot = len(tail_along)
        tail_along[slot] = links.start(tails(me.zo(off)), tail_along_in.at[slot], me.at(z=me.zo(step)))

    tail_send(3, 1)
    tail_send(5, -1)
    tail_send(4, 2 * me.d)
    for i, off in enumerate(order):
        k = 1 if i % 2 == 0 else -1
        hops[i] = links.start(head(me.xo(2), me.zo(off)), cross_in.at[0, off], me.at(x=me.xo(k)))
        direct[i] = links.start(head(me.xo(-k), me.zo(off)), cross_in.at[1, off], me.at(x=me.xo(-k)))

    def relay(i):
        off = order[i]
        k = 1 if i % 2 == 0 else -1
        hops[i].wait_recv()
        add_to(head(me.xo(k), me.zo(off)), cross_in.at[0, off])
        relayed[i] = links.start(head(me.xo(k), me.zo(off)), cross_in.at[2, off], me.at(x=me.xo(k)))

    def collect(i):
        off = order[i]
        direct[i].wait_recv()
        relayed[i].wait_recv()
        add_to(head(x, me.zo(off)), cross_in.at[1, off], cross_in.at[2, off])
        if off:
            along[off] = links.start(head(x, me.zo(off)), along_in.at[off - 1], me.at(z=me.zo(off)))

    for i in range(8):
        relay(i)
        if i == 3:
            for copy in list(tail_along.values()):
                copy.wait_recv()
            add_to(tails(me.zo(2)), tail_along_in.at[0])
            add_to(tails(me.zo(-2)), tail_along_in.at[1])
            add_to(tails(me.zo(2 * me.d)), tail_along_in.at[2])
            for step in (2, -2, 1, -1):
                tail_send(step, step)
        if i >= 2:
            collect(i - 2)
    for slot in range(3, 7):
        tail_along[slot].wait_recv()
    add_to(tails(z), *[tail_along_in.at[i] for i in range(3, 7)])
    for k in (2, 1, 3):
        tail_cross[k] = links.start(tail(me.xo(k)), tail_cross_in.at[k - 1], me.at(x=me.xo(k)))
    for i in range(6, 8):
        collect(i)
    for off in FAR:
        along[off].wait_recv()
    total = head(x, z)[...].astype(F32)
    for i in range(7):
        total = total + along_in[i].astype(F32)
    result[pl.ds(0, HEAD)] = total
    for k in (2, 1, 3):
        tail_cross[k].wait_recv()
    total = tail(x)[...].astype(F32)
    for i in range(3):
        total = total + tail_cross_in[i].astype(F32)
    result[pl.ds(HEAD, TAIL)] = total


def first_weights(w_first, gate_hbm, in_hbm):
    return [(gate_hbm, w_first.at[pl.ds(0, UNITS)]), (in_hbm, w_first.at[pl.ds(UNITS, UNITS)])]


def contract(a, b):
    return lax.dot_general(a, b, (((0,), (0,)), ((), ())), preferred_element_type=F32)


def gelu(v):
    return jax.nn.gelu(v)


def scale_columns(weights, gain_ref, first_row, first, count):
    def step(i, carry):
        columns = pl.ds(pl.multiple_of((first + i) * 128, 128), 128)
        line = gain_ref[pl.ds(first_row + first + i, 1), :]
        weights[:, columns] = (weights[:, columns].astype(F32) * line).astype(BF16)
        return carry

    lax.fori_loop(0, count, step, 0)


def greet(senders, extra=None):
    barrier = pltpu.get_barrier_semaphore()
    for device in senders:
        pl.semaphore_signal(barrier, inc=1, device_id=device, device_id_type=MESH)
    if extra is not None:
        extra(barrier)
    return barrier


def encoder_kernel(
    tokens_ref, history_ref, ids_ref, language_ref, gain_ref, gate_hbm, in_hbm, out_hbm,
    all_ref, pair_ref, languages_ref, branch_ref,
    turned, column, base, blocks, w_first, w_out, pre_send, relay_in, pre_in, pre_own,
    squares, squares_in, squares_core, hidden, lang_send, fan_out, memory_all, lang_all,
    sums, theirs, cross_in, along_in, tail_along_in, tail_cross_in, result,
    send_sem, recv_sem, turn_sem, wide_send, wide_recv, fan_send, fan_recv, load_sem,
):
    me = Place()
    x, y, z, c = me.x, me.y, me.z, me.c
    links = Links(send_sem, recv_sem)
    diagonal = x == y

    loads = [
        pltpu.make_async_copy(src, dst, load_sem.at[i])
        for i, (src, dst) in enumerate(first_weights(w_first, gate_hbm, in_hbm) + [(out_hbm, w_out)])
    ]
    for load in loads:
        load.start()

    def fan(barrier):
        for k in range(4):
            for device in (me.at(x=y, y=me.yo(k)), me.at(x=me.xo(k), y=x)):
                if k:
                    pl.semaphore_signal(barrier, inc=1, device_id=device, device_id_type=MESH)
                else:
                    @pl.when(jnp.logical_not(diagonal))
                    def _():
                        pl.semaphore_signal(barrier, inc=1, device_id=device, device_id_type=MESH)

    barrier = greet(me.plane() + me.column(), fan)
    turned[0] = tokens_ref[...].reshape(256, PART).T
    for e in range(4):
        turned[1, :, pl.ds(e * SEQ, SEQ)] = history_ref[ids_ref[e]].T
    lane = lax.broadcasted_iota(jnp.int32, (8, 128), 1)
    lines = jnp.zeros((8, 128), jnp.int32)
    for e in range(4):
        lines = jnp.where(lane == e, language_ref[e], lines)
    lang_send[...] = lines

    pl.semaphore_wait(barrier, jnp.where(diagonal, 20, 22))

    other = me.at(y=x, x=y)
    turn = pltpu.make_async_remote_copy(
        src_ref=turned.at[1], dst_ref=base, send_sem=turn_sem.at[0, 0], recv_sem=turn_sem.at[1, 0],
        device_id=other, device_id_type=MESH)

    def meanwhile():
        @pl.when(jnp.logical_not(diagonal))
        def _():
            turn.start()

        @pl.when(diagonal)
        def _():
            base[...] = turned[1]

        loads[0].wait()
        loads[1].wait()
        scale_columns(w_first, gain_ref, y * 10, 0, 10)

    lang_copies = [links.start(lang_send, lang_all.at[y], me.at(y=me.yo(k))) for k in (1, 2, 3)]

    finish_gather = gather_turned(
        links, me, blocks, turned.at[0], column, wide_send, wide_recv, meanwhile)

    ones = jnp.ones((8, 256), F32)

    def products(g):
        product = jnp.dot(w_first[...], blocks[g].reshape(SLICE, 256), preferred_element_type=F32)
        return product[:UNITS], product[UNITS:]

    def measure(g):
        wide = blocks[g, :, c].astype(F32).reshape(SLICE // 2, 256)
        squares[g] = ones * jnp.sum(wide * wide, axis=0, keepdims=True)

    up, down, far = me.yo(1), me.yo(-1), me.yo(2)
    to_up, to_down, to_far = me.at(y=up), me.at(y=down), me.at(y=far)
    gate, value = products(far)
    pre_send[far, 0] = gate.astype(BF16)
    relay_gate = links.start(pre_send.at[far, 0], relay_in.at[0], to_up)
    pre_send[far, 1] = value.astype(BF16)
    relay_value = links.start(pre_send.at[far, 1], relay_in.at[1], to_down)
    measure(far)
    square_copies = [links.start(squares.at[far], squares_in.at[0], to_far)]
    gate, value = products(up)
    pre_send[up, 0] = gate.astype(BF16)
    pre_send[up, 1] = value.astype(BF16)
    straight_up = links.start(pre_send.at[up, 1], pre_in.at[0, 1], to_up)
    measure(up)
    square_copies.append(links.start(squares.at[up], squares_in.at[1], to_up))
    gate, value = products(down)
    pre_send[down, 0] = gate.astype(BF16)
    straight_down = links.start(pre_send.at[down, 0], pre_in.at[1, 0], to_down)
    pre_send[down, 1] = value.astype(BF16)
    measure(down)
    square_copies.append(links.start(squares.at[down], squares_in.at[2], to_down))
    relay_gate.wait_recv()
    add_to(pre_send.at[up, 0], relay_in.at[0])
    joint_up = links.start(pre_send.at[up, 0], pre_in.at[0, 0], to_up)
    relay_value.wait_recv()
    add_to(pre_send.at[down, 1], relay_in.at[1])
    joint_down = links.start(pre_send.at[down, 1], pre_in.at[1, 1], to_down)
    gate, value = products(y)
    measure(y)
    pre_own[0] = gate
    pre_own[1] = value
    for copy in lang_copies:
        copy.wait_recv()
    lang_all[y] = lang_send[...]
    for g in range(4):
        names = lang_all[g].astype(F32)
        for e in range(4):
            name = jnp.max(jnp.where(lane == e, names, 0.0)).astype(jnp.int32)
            languages_ref[g * 4 + e] = name
    most = jnp.int32(0)
    for l in range(4):
        load = jnp.int32(0)
        for i in range(16):
            load = load + (languages_ref[i] == l).astype(jnp.int32)
        most = jnp.maximum(most, load)
    branch_ref[0] = (most > 4).astype(jnp.int32) + (most > 6).astype(jnp.int32)
    for copy in square_copies:
        copy.wait_recv()
    squares_core[0] = squares[y] + squares_in[0] + squares_in[1] + squares_in[2]
    core_square = links.start(squares_core.at[0], squares_core.at[1], me.at(c=1 - c))
    core_square.wait_recv()
    total = squares_core[0] + squares_core[1]
    inverse = lax.rsqrt(total * (1.0 / WIDTH) + EPS)[0:1, :]
    straight_up.wait_recv()
    straight_down.wait_recv()
    joint_up.wait_recv()
    joint_down.wait_recv()
    gate = (pre_own[0] + pre_in[0, 0].astype(F32) + pre_in[1, 0].astype(F32)) * inverse
    value = (pre_own[1] + pre_in[0, 1].astype(F32) + pre_in[1, 1].astype(F32)) * inverse
    hidden[y] = (gelu(gate) * value).astype(BF16)

    half = UNITS // 2
    low, high = pl.ds(0, half), pl.ds(half, half)

    def units(g, part, device):
        return links.start(hidden.at[g, part], hidden.at[g, part], device)

    low_up, high_down = units(y, low, to_up), units(y, high, to_down)
    high_up, low_down = units(y, high, to_up), units(y, low, to_down)
    loads[2].wait()
    partner = me.at(c=1 - c)
    core_copies = []

    def outward(g):
        sums[g] = contract(w_out[...], hidden[g]).astype(BF16).reshape(NZ, 2, PART, 256)
        core_copies.append((g, links.start(sums.at[g, :, 1 - c], theirs.at[g], partner)))

    def join():
        g, copy = core_copies.pop(0)
        copy.wait_recv()
        add_to(sums.at[g, :, c], theirs.at[g])

    outward(y)
    low_up.wait_recv()
    far_up = units(down, low, to_up)
    high_down.wait_recv()
    far_down = units(up, high, to_down)
    high_up.wait_recv()
    outward(down)
    low_down.wait_recv()
    outward(up)
    for _ in range(3):
        join()
    far_up.wait_recv()
    far_down.wait_recv()
    outward(far)

    scatter_plane(
        links, me,
        (sums, theirs, cross_in, along_in, tail_along_in, tail_cross_in, result),
        core_copies,
    )

    @pl.when(jnp.logical_not(diagonal))
    def _():
        turn.wait_recv()

    encoded = (blocks[x, z, c].astype(F32) + result[...]).astype(BF16)
    baseline = base[...].astype(F32)
    difference = encoded.astype(F32) - baseline
    example = lax.broadcasted_iota(jnp.int32, (PART, 256), 1) // SEQ
    size = jnp.abs(difference)
    scale = jnp.zeros((PART, 256), F32)
    for e in range(4):
        top = jnp.max(jnp.where(example == e, size, 0.0), axis=1, keepdims=True) + EPS
        scale = jnp.where(example == e, top, scale)
    codes = (difference / scale).astype(BF16)
    memory = (baseline + codes.astype(F32) * scale).astype(BF16)
    pair_ref[0] = memory
    pair_ref[1] = codes

    slot_lane = lax.broadcasted_iota(jnp.int32, (SEQ, PAIR), 1)
    slot_line = lax.broadcasted_iota(jnp.int32, (SEQ, PAIR), 0)
    for l in range(4):
        count, picks = jnp.int32(0), []
        for e in range(4):
            named = languages_ref[x * 4 + e] == l
            start = jnp.where(named, count * SEQ, -SEQ)
            count = count + named.astype(jnp.int32)
            picks.append((slot_lane == slot_line + start).astype(F32).astype(BF16))
        picked = jnp.dot(memory, jnp.concatenate(picks, axis=0), preferred_element_type=F32)
        fan_out[l] = picked.astype(BF16)

    def fan_copy(l, g):
        return pltpu.make_async_remote_copy(
            src_ref=fan_out.at[l], dst_ref=memory_all.at[g], send_sem=fan_send.at[l], recv_sem=fan_recv.at[g],
            device_id=me.at(y=l, x=y), device_id_type=MESH)

    fans = [fan_copy(l, x) for l in range(4)]
    arrivals = [fan_copy(g, g) for g in range(4)]
    for l in range(4):
        @pl.when(jnp.logical_not(jnp.logical_and(diagonal, y == l)))
        def _():
            fans[l].start()

    @pl.when(diagonal)
    def _():
        memory_all[x] = fan_out[y]

    for g in range(4):
        @pl.when(jnp.logical_not(jnp.logical_and(diagonal, x == g)))
        def _():
            arrivals[g].wait_recv()

    all_ref[...] = memory_all[...]

    for l in range(4):
        @pl.when(jnp.logical_not(jnp.logical_and(diagonal, y == l)))
        def _():
            fans[l].wait_send()

    @pl.when(jnp.logical_not(diagonal))
    def _():
        turn.wait_send()

    finish_gather()
    links.finish()


def decoder_kernel(
    rows, memory_ref, pair_ref, language_ref, gain_ref, gate_hbm, in_hbm, out_hbm,
    decoded_ref, new_memory_ref, quantized_ref,
    blocks, own, w_first, w_out, hidden, acc, squares, finished, home,
    sums, theirs, cross_in, along_in, tail_along_in, tail_cross_in, result,
    send_sem, recv_sem, turn_sem, load_sem,
):
    me = Place()
    x, y, z, c = me.x, me.y, me.z, me.c
    links = Links(send_sem, recv_sem)
    diagonal = x == y
    other = me.at(y=x, x=y)

    def greet_other(barrier):
        @pl.when(jnp.logical_not(diagonal))
        def _():
            pl.semaphore_signal(barrier, inc=1, device_id=other, device_id_type=MESH)

    barrier = greet(me.plane() + me.column(), greet_other)
    loads = [
        pltpu.make_async_copy(src, dst, load_sem.at[i])
        for i, (src, dst) in enumerate(first_weights(w_first, gate_hbm, in_hbm) + [(out_hbm, w_out)])
    ]
    for load in loads:
        load.start()

    lane = lax.broadcasted_iota(jnp.int32, (SEQ, rows), 1)
    line = lax.broadcasted_iota(jnp.int32, (SEQ, rows), 0)
    number = jnp.int32(0)
    chosen = jnp.zeros((PART, rows), F32)
    for g in range(4):
        count = jnp.int32(0)
        for e in range(4):
            count = count + (language_ref[g * 4 + e] == y).astype(jnp.int32)
        picks = []
        for j in range(2):
            start = jnp.where(count > j, (number + j) * SEQ, -SEQ)
            picks.append((lane == line + start).astype(F32).astype(BF16))
        number = number + count
        chosen = chosen + jnp.dot(memory_ref[g], jnp.concatenate(picks, axis=0), preferred_element_type=F32)
    own[...] = chosen.astype(BF16)
    blocks[x, z, c] = own[...]

    pl.semaphore_wait(barrier, jnp.where(diagonal, 14, 15))

    turn = pltpu.make_async_remote_copy(
        src_ref=pair_ref, dst_ref=home, send_sem=turn_sem.at[0], recv_sem=turn_sem.at[1],
        device_id=other, device_id_type=MESH)

    def meanwhile(i):
        if i == 0:
            @pl.when(jnp.logical_not(diagonal))
            def _():
                turn.start()

            @pl.when(diagonal)
            def _():
                home[...] = pair_ref[...]

            loads[0].wait()
            loads[1].wait()
        scale_columns(w_first, gain_ref, 0, 5 * i, 5)

    squares[0] = jnp.zeros((8, rows), F32)

    def seen(ref):
        wide = ref[...].astype(F32)
        squares[0] = squares[0] + jnp.sum(wide * wide, axis=(0, 1))[None, :]

    gather_plane(links, me, blocks, meanwhile, seen)
    partner = me.at(c=1 - c)
    core_square = links.start(squares.at[0], squares.at[1], partner)
    for g in range(4):
        part = pl.ds(g * SLICE, SLICE)
        term = jnp.dot(w_first[:, part], blocks[g].reshape(SLICE, rows), preferred_element_type=F32)
        acc[...] = term if g == 0 else acc[...] + term
    core_square.wait_recv()
    inverse = lax.rsqrt((squares[0] + squares[1]) * (1.0 / WIDTH) + EPS)[0:1, :]
    hidden[...] = (gelu(acc[:UNITS] * inverse) * (acc[UNITS:] * inverse)).astype(BF16)

    loads[2].wait()
    core_copies = []
    for k in (2, 1, 3, 0):
        g = me.xo(k)
        columns = pl.ds(pl.multiple_of(g * SLICE, 128), SLICE)
        product = contract(w_out[:, columns], hidden[...])
        sums[g] = product.astype(BF16).reshape(NZ, 2, PART, rows)
        core_copies.append((g, links.start(sums.at[g, :, 1 - c], theirs.at[g], partner)))
    scatter_plane(
        links, me,
        (sums, theirs, cross_in, along_in, tail_along_in, tail_cross_in, result),
        core_copies,
    )
    finished[y] = (own[...].astype(F32) + result[...]).astype(BF16)
    returns = [links.start(finished.at[y], finished.at[y], me.at(y=me.yo(k))) for k in (1, 2, 3)]

    place = lax.broadcasted_iota(jnp.int32, (rows, 256), 0)
    column = lax.broadcasted_iota(jnp.int32, (rows, 256), 1)
    example, token = column // SEQ, column % SEQ
    sources = []
    for l in range(4):
        source = jnp.full((rows, 256), -1, jnp.int32)
        for e in range(4):
            lang = language_ref[y * 4 + e]
            slot = jnp.int32(0)
            for i in range(16):
                ahead = jnp.logical_and(language_ref[i] == lang, i < y * 4 + e)
                slot = slot + ahead.astype(jnp.int32)
            start = jnp.where(lang == l, slot * SEQ, -SEQ)
            source = jnp.where(example == e, token + start, source)
        sources.append((place == source).astype(F32).astype(BF16))

    @pl.when(jnp.logical_not(diagonal))
    def _():
        turn.wait_recv()

    new_memory_ref[...] = home[0].T.reshape(4, SEQ, PART)
    quantized_ref[...] = home[1].T.reshape(4, SEQ, PART)
    for copy in returns:
        copy.wait_recv()
    answer = jnp.zeros((PART, 256), F32)
    for l in range(4):
        answer = answer + jnp.dot(finished[l], sources[l], preferred_element_type=F32)
    decoded_ref[...] = answer.astype(BF16).T.reshape(4, SEQ, PART)

    @pl.when(jnp.logical_not(diagonal))
    def _():
        turn.wait_send()

    links.finish()


VMEM = pl.BlockSpec(memory_space=pltpu.VMEM)
SMEM = pl.BlockSpec(memory_space=pltpu.SMEM)
ANY = pl.BlockSpec(memory_space=pl.ANY)
DMA = pltpu.SemaphoreType.DMA


def encode(tokens, history, ids, language, gain, gate, up, out):
    sds = jax.ShapeDtypeStruct
    return pl.pallas_call(
        encoder_kernel,
        out_shape=(
            sds((4, PART, PAIR), BF16),
            sds((2, PART, 256), BF16),
            sds((16,), jnp.int32),
            sds((1,), jnp.int32),
        ),
        in_specs=[VMEM, VMEM, SMEM, SMEM, VMEM, ANY, ANY, ANY],
        out_specs=(VMEM, VMEM, SMEM, SMEM),
        scratch_shapes=[
            pltpu.VMEM((2, PART, 256), BF16),
            pltpu.VMEM((NZ, HEAD, 256), BF16),
            pltpu.VMEM((PART, 256), BF16),
            pltpu.VMEM((NX, NZ, 2, PART, 256), BF16),
            pltpu.VMEM((2 * UNITS, SLICE), BF16),
            pltpu.VMEM((UNITS, SLICE), BF16),
            pltpu.VMEM((4, 2, UNITS, 256), BF16),
            pltpu.VMEM((2, UNITS, 256), BF16),
            pltpu.VMEM((2, 2, UNITS, 256), BF16),
            pltpu.VMEM((2, UNITS, 256), F32),
            pltpu.VMEM((4, 8, 256), F32),
            pltpu.VMEM((3, 8, 256), F32),
            pltpu.VMEM((2, 8, 256), F32),
            pltpu.VMEM((4, UNITS, 256), BF16),
            pltpu.VMEM((8, 128), jnp.int32),
            pltpu.VMEM((4, PART, PAIR), BF16),
            pltpu.VMEM((4, PART, PAIR), BF16),
            pltpu.VMEM((4, 8, 128), jnp.int32),
            *scatter_shapes(256),
            DMA((COPIES,)),
            DMA((COPIES,)),
            DMA((2, 1)),
            DMA((9, 4)),
            DMA((9, 4)),
            DMA((4,)),
            DMA((4,)),
            DMA((3,)),
        ],
        compiler_params=pltpu.CompilerParams(
            collective_id=0, has_side_effects=True, vmem_limit_bytes=56 << 20
        ),
    )(tokens, history, ids, language, gain, gate, up, out)


def decode(rows, number, memory, pair, language, gain, gate, up, out):
    return pl.pallas_call(
        functools.partial(decoder_kernel, rows),
        out_shape=(jax.ShapeDtypeStruct((4, SEQ, PART), BF16),) * 3,
        in_specs=[VMEM, VMEM, SMEM, VMEM, ANY, ANY, ANY],
        out_specs=(VMEM, VMEM, VMEM),
        scratch_shapes=[
            pltpu.VMEM((NX, NZ, 2, PART, rows), BF16),
            pltpu.VMEM((PART, rows), BF16),
            pltpu.VMEM((2 * UNITS, WIDTH), BF16),
            pltpu.VMEM((UNITS, WIDTH), BF16),
            pltpu.VMEM((UNITS, rows), BF16),
            pltpu.VMEM((2 * UNITS, rows), F32),
            pltpu.VMEM((2, 8, rows), F32),
            pltpu.VMEM((4, PART, rows), BF16),
            pltpu.VMEM((2, PART, 256), BF16),
            *scatter_shapes(rows),
            DMA((COPIES,)),
            DMA((COPIES,)),
            DMA((2,)),
            DMA((3,)),
        ],
        compiler_params=pltpu.CompilerParams(
            collective_id=number, has_side_effects=True, vmem_limit_bytes=56 << 20
        ),
    )(memory, pair, language, gain, gate, up, out)


def shards(
    tokens, language, example_ids, history, enc_gain, dec_gain, enc_gate, enc_in, enc_out, dec_gate, dec_in, dec_out
):
    memory_all, pair, languages, branch = encode(
        tokens, history, example_ids, language.reshape(4), enc_gain.reshape(40, 128), enc_gate.T, enc_in.T, enc_out
    )
    return lax.switch(
        branch[0],
        [functools.partial(decode, rows * SEQ, number) for number, rows in ((1, 4), (2, 6), (3, 8))],
        memory_all, pair, languages, dec_gain.reshape(40, 128), dec_gate[0].T, dec_in[0].T, dec_out[0],
    )


def solution(mesh):
    in_specs = (
        P("section", None, "tp"),
        P("section", None),
        P("section"),
        P(None, None, "tp"),
        P(),
        P("section", None),
        P("section", "tp"),
        P("section", "tp"),
        P("tp", "section"),
        P("section", None, "tp"),
        P("section", None, "tp"),
        P("section", "tp", None),
    )
    out_specs = (P("section", None, "tp"), P("section", None, "tp"), P("section", None, "tp"))
    return jax.shard_map(shards, mesh=mesh, in_specs=in_specs, out_specs=out_specs, check_vma=False)
```

```python
import functools

import jax
import jax.numpy as jnp
from jax import lax
from jax.experimental import pallas as pl
from jax.experimental.pallas import tpu as pltpu
from jax.sharding import PartitionSpec as P

MESH = pl.DeviceIdType.MESH
BF16 = jnp.bfloat16
F32 = jnp.float32
EPS = 1e-06
NX, NZ, NY = 4, 8, 4
SEQ = 64
PART = 80
HEAD = 64
TAIL = PART - HEAD
TURN_HEAD = 48
TURN_TAIL = PART - TURN_HEAD
SLICE = 1280
UNITS = 320
WIDTH = 5120
COPIES = 128
PAIR = 2 * SEQ


class Links:
    def __init__(self, send_sem, recv_sem):
        self.send_sem, self.recv_sem = send_sem, recv_sem
        self.count = 0
        self.sent = []

    def start(self, src, dst, device):
        copy = pltpu.make_async_remote_copy(
            src_ref=src,
            dst_ref=dst,
            send_sem=self.send_sem.at[self.count],
            recv_sem=self.recv_sem.at[self.count],
            device_id=device,
            device_id_type=MESH,
        )
        self.count += 1
        copy.start()
        self.sent.append(copy)
        return copy

    def finish(self):
        for copy in self.sent:
            copy.wait_send()
        self.sent = []


class Place:
    def __init__(self):
        self.y = lax.axis_index("section")
        t = lax.axis_index("tp")
        self.x, self.z, self.c = t // 16, (t // 2) % 8, t % 2
        self.d = 1 - 2 * self.c

    def at(self, y=None, x=None, z=None, c=None):
        y = self.y if y is None else y
        x = self.x if x is None else x
        z = self.z if z is None else z
        c = self.c if c is None else c
        return (y, (x * 8 + z) * 2 + c)

    def xo(self, off):
        return (self.x + off + 8) % 4

    def yo(self, off):
        return (self.y + off + 8) % 4

    def zo(self, off):
        return (self.z + off + 8) % 8

    def plane(self):
        others = [self.at(z=self.zo(off)) for off in NEAR]
        others += [self.at(x=self.xo(k)) for k in (1, 2, 3)]
        return others + [self.at(c=1 - self.c)]

    def column(self):
        return [self.at(y=self.yo(k)) for k in (1, 2, 3)]


NEAR = (1, 7, 2, 6, 3, 5, 4)
FAR = (4, 3, 5, 2, 6, 1, 7)


class TailAlong:
    def __init__(self, links, me, tails, landed):
        self.links, self.me, self.tails, self.landed = links, me, tails, landed
        self.copies = {}

    def send(self, off, source, step):
        ref = self.tails(self.me.zo(source))
        self.copies[off] = self.links.start(ref, ref, self.me.at(z=self.me.zo(step)))

    def begin(self):
        for off in (2, 6, 1, 7):
            self.send(off, 0, off)
        self.landed(self.tails(self.me.z))

    def arrive(self, off):
        self.copies[off].wait_recv()
        self.landed(self.tails(self.me.zo(-off)))

    def relay(self):
        self.arrive(2)
        self.send(3, -2, 1)
        self.arrive(6)
        self.send(5, 2, -1)
        self.send(4, 2 * self.me.d, -2 * self.me.d)

    def finish(self):
        for off in (1, 7, 3, 5, 4):
            self.arrive(off)


def gather_plane(links, me, blocks, meanwhile, seen):
    x, z, c = me.x, me.z, me.c
    partner = me.at(c=1 - c)

    def head(xx, zz):
        return blocks.at[xx, zz, c, pl.ds(0, HEAD)]

    def tail(xx):
        return blocks.at[xx, z, c, pl.ds(HEAD, TAIL)]

    def heads(zz):
        return blocks.at[:, zz, c, pl.ds(0, HEAD)]

    def tails(zz):
        return blocks.at[:, zz, c, pl.ds(HEAD, TAIL)]

    def send(ref, device):
        return links.start(ref, ref, device)

    core = []

    def to_core(ref):
        core.append(send(ref, partner))
        seen(ref)

    tail_along = TailAlong(links, me, tails, to_core)
    tail_cross = [send(tail(x), me.at(x=me.xo(k))) for k in (1, 2, 3)]
    order = (0,) + NEAR
    cross, second = {}, {}

    def send_cross(off):
        block = head(x, me.zo(-off))
        cross[off] = [send(block, me.at(x=me.xo(k))) for k in (1, 3)]

    def hop(i):
        off = order[i]
        for copy in cross[off]:
            copy.wait_recv()
        k = 1 if i % 2 == 0 else -1
        second[off] = send(head(me.xo(-k), me.zo(-off)), me.at(x=me.xo(k)))

    def land(i):
        off = order[i]
        second[off].wait_recv()
        to_core(heads(me.zo(-off)))

    along = {off: send(head(x, z), me.at(z=me.zo(off))) for off in NEAR}
    send_cross(0)
    for i in range(1, 8):
        meanwhile(i - 1)
        along[order[i]].wait_recv()
        send_cross(order[i])
        if i == 2:
            for copy in tail_cross:
                copy.wait_recv()
            tail_along.begin()
        if i >= 3:
            hop(i - 3)
        if i == 6:
            tail_along.relay()
    meanwhile(7)
    for i in range(5, 8):
        land(i - 5)
        hop(i)
    for i in range(3, 8):
        land(i)
    tail_along.finish()
    for copy in core:
        copy.wait_recv()


def gather_turned(links, me, blocks, own, column, fan_send, fan_recv, meanwhile):
    x, y, z, c = me.x, me.y, me.z, me.c
    partner = me.at(c=1 - c)
    diagonal = x == y

    def fan(stage, src, dst):
        copies = []
        for k in range(4):
            copies.append(pltpu.make_async_remote_copy(
                src_ref=src, dst_ref=dst, send_sem=fan_send.at[stage, k], recv_sem=fan_recv.at[stage, y],
                device_id=me.at(x=me.xo(k), y=x), device_id_type=MESH))

        @pl.when(jnp.logical_not(diagonal))
        def _():
            copies[0].start()

        @pl.when(diagonal)
        def _():
            dst[...] = src[...]

        for copy in copies[1:]:
            copy.start()
        arrivals = []
        for j in range(4):
            g = me.yo(j)
            arrivals.append(pltpu.make_async_remote_copy(
                src_ref=src, dst_ref=dst, send_sem=fan_send.at[stage, j], recv_sem=fan_recv.at[stage, g],
                device_id=me.at(x=me.xo(1), y=x), device_id_type=MESH))
        return copies, arrivals

    def land(fans):
        @pl.when(jnp.logical_not(diagonal))
        def _():
            fans[1][0].wait_recv()

        for copy in fans[1][1:]:
            copy.wait_recv()

    def send(src, dst, device):
        return links.start(src, dst, device)

    def heads(zz):
        return blocks.at[:, zz, c, pl.ds(0, TURN_HEAD)]

    def tails(zz):
        return blocks.at[:, zz, c, pl.ds(TURN_HEAD, TURN_TAIL)]

    first = own.at[pl.ds(0, TURN_HEAD)]
    tail_fan = fan(8, own.at[pl.ds(TURN_HEAD, TURN_TAIL)], blocks.at[y, z, c, pl.ds(TURN_HEAD, TURN_TAIL)])
    along = {off: send(first, column.at[z], me.at(z=me.zo(off))) for off in NEAR}
    fans = {0: fan(0, first, blocks.at[y, z, c, pl.ds(0, TURN_HEAD)])}
    meanwhile()
    core = []

    def to_core(ref):
        core.append(send(ref, ref, partner))

    tail_along = TailAlong(links, me, tails, to_core)
    for i, off in enumerate(NEAR):
        along[off].wait_recv()
        zz = me.zo(-off)
        fans[off] = fan(i + 1, column.at[zz], blocks.at[y, zz, c, pl.ds(0, TURN_HEAD)])
        if i == 1:
            land(tail_fan)
            tail_along.begin()
    for i, off in enumerate((0,) + NEAR):
        land(fans[off])
        to_core(heads(me.zo(-off)))
        if i == 2:
            tail_along.relay()
    tail_along.finish()
    for copy in core:
        copy.wait_recv()

    def finish():
        for copies, _ in [tail_fan] + [fans[off] for off in (0,) + NEAR]:
            @pl.when(jnp.logical_not(diagonal))
            def _():
                copies[0].wait_send()

            for copy in copies[1:]:
                copy.wait_send()

    return finish


def add_to(dst, *terms):
    total = dst[...].astype(F32)
    for term in terms:
        total = total + term[...].astype(F32)
    dst[...] = total.astype(dst.dtype)


def scatter_shapes(rows):
    return [
        pltpu.VMEM((NX, NZ, 2, PART, rows), BF16),
        pltpu.VMEM((NX, NZ, PART, rows), BF16),
        pltpu.VMEM((3, NZ, HEAD, rows), BF16),
        pltpu.VMEM((7, HEAD, rows), BF16),
        pltpu.VMEM((7, NX, TAIL, rows), BF16),
        pltpu.VMEM((3, TAIL, rows), BF16),
        pltpu.VMEM((PART, rows), F32),
    ]


def scatter_plane(links, me, bufs, parts):
    sums, theirs, cross_in, along_in, tail_along_in, tail_cross_in, result = bufs
    x, z, c = me.x, me.z, me.c

    def head(xx, zz):
        return sums.at[xx, zz, c, pl.ds(0, HEAD)]

    def tail(xx):
        return sums.at[xx, z, c, pl.ds(HEAD, TAIL)]

    def tails(zz):
        return sums.at[:, zz, c, pl.ds(HEAD, TAIL)]

    for xx, copy in parts:
        copy.wait_recv()
        add_to(sums.at[xx, :, c], theirs.at[xx])

    order = FAR + (0,)
    hops, direct, relayed, along, tail_along, tail_cross = {}, {}, {}, {}, {}, {}

    def tail_send(off, step):
        slot = len(tail_along)
        tail_along[slot] = links.start(tails(me.zo(off)), tail_along_in.at[slot], me.at(z=me.zo(step)))

    tail_send(3, 1)
    tail_send(5, -1)
    tail_send(4, 2 * me.d)
    for i, off in enumerate(order):
        k = 1 if i % 2 == 0 else -1
        hops[i] = links.start(head(me.xo(2), me.zo(off)), cross_in.at[0, off], me.at(x=me.xo(k)))
        direct[i] = links.start(head(me.xo(-k), me.zo(off)), cross_in.at[1, off], me.at(x=me.xo(-k)))

    def relay(i):
        off = order[i]
        k = 1 if i % 2 == 0 else -1
        hops[i].wait_recv()
        add_to(head(me.xo(k), me.zo(off)), cross_in.at[0, off])
        relayed[i] = links.start(head(me.xo(k), me.zo(off)), cross_in.at[2, off], me.at(x=me.xo(k)))

    def collect(i):
        off = order[i]
        direct[i].wait_recv()
        relayed[i].wait_recv()
        add_to(head(x, me.zo(off)), cross_in.at[1, off], cross_in.at[2, off])
        if off:
            along[off] = links.start(head(x, me.zo(off)), along_in.at[off - 1], me.at(z=me.zo(off)))

    for i in range(8):
        relay(i)
        if i == 3:
            for copy in list(tail_along.values()):
                copy.wait_recv()
            add_to(tails(me.zo(2)), tail_along_in.at[0])
            add_to(tails(me.zo(-2)), tail_along_in.at[1])
            add_to(tails(me.zo(2 * me.d)), tail_along_in.at[2])
            for step in (2, -2, 1, -1):
                tail_send(step, step)
        if i >= 2:
            collect(i - 2)
    for slot in range(3, 7):
        tail_along[slot].wait_recv()
    add_to(tails(z), *[tail_along_in.at[i] for i in range(3, 7)])
    for k in (2, 1, 3):
        tail_cross[k] = links.start(tail(me.xo(k)), tail_cross_in.at[k - 1], me.at(x=me.xo(k)))
    for i in range(6, 8):
        collect(i)
    for off in FAR:
        along[off].wait_recv()
    total = head(x, z)[...].astype(F32)
    for i in range(7):
        total = total + along_in[i].astype(F32)
    result[pl.ds(0, HEAD)] = total
    for k in (2, 1, 3):
        tail_cross[k].wait_recv()
    total = tail(x)[...].astype(F32)
    for i in range(3):
        total = total + tail_cross_in[i].astype(F32)
    result[pl.ds(HEAD, TAIL)] = total


def first_weights(w_first, gate_hbm, in_hbm):
    return [(gate_hbm, w_first.at[pl.ds(0, UNITS)]), (in_hbm, w_first.at[pl.ds(UNITS, UNITS)])]


def contract(a, b):
    return lax.dot_general(a, b, (((0,), (0,)), ((), ())), preferred_element_type=F32)


def gelu(v):
    return jax.nn.gelu(v)


def scale_columns(weights, gain_ref, first_row, first, count):
    def step(i, carry):
        columns = pl.ds(pl.multiple_of((first + i) * 128, 128), 128)
        line = gain_ref[pl.ds(first_row + first + i, 1), :]
        weights[:, columns] = (weights[:, columns].astype(F32) * line).astype(BF16)
        return carry

    lax.fori_loop(0, count, step, 0)


def greet(senders, extra=None):
    barrier = pltpu.get_barrier_semaphore()
    for device in senders:
        pl.semaphore_signal(barrier, inc=1, device_id=device, device_id_type=MESH)
    if extra is not None:
        extra(barrier)
    return barrier


def encoder_kernel(
    tokens_ref, history_ref, ids_ref, language_ref, gain_ref, gate_hbm, in_hbm, out_hbm,
    all_ref, pair_ref, languages_ref, branch_ref,
    turned, column, base, blocks, w_first, w_out, pre_send, relay_in, pre_in, pre_own,
    squares, squares_in, squares_core, hidden, lang_send, fan_out, memory_all, lang_all,
    sums, theirs, cross_in, along_in, tail_along_in, tail_cross_in, result,
    send_sem, recv_sem, turn_sem, wide_send, wide_recv, fan_send, fan_recv, load_sem,
):
    me = Place()
    x, y, z, c = me.x, me.y, me.z, me.c
    links = Links(send_sem, recv_sem)
    diagonal = x == y

    loads = [
        pltpu.make_async_copy(src, dst, load_sem.at[i])
        for i, (src, dst) in enumerate(first_weights(w_first, gate_hbm, in_hbm) + [(out_hbm, w_out)])
    ]
    for load in loads:
        load.start()

    def fan(barrier):
        for k in range(4):
            for device in (me.at(x=y, y=me.yo(k)), me.at(x=me.xo(k), y=x)):
                if k:
                    pl.semaphore_signal(barrier, inc=1, device_id=device, device_id_type=MESH)
                else:
                    @pl.when(jnp.logical_not(diagonal))
                    def _():
                        pl.semaphore_signal(barrier, inc=1, device_id=device, device_id_type=MESH)

    barrier = greet(me.plane() + me.column(), fan)
    turned[0] = tokens_ref[...].reshape(256, PART).T
    for e in range(4):
        turned[1, :, pl.ds(e * SEQ, SEQ)] = history_ref[ids_ref[e]].T
    lane = lax.broadcasted_iota(jnp.int32, (8, 128), 1)
    lines = jnp.zeros((8, 128), jnp.int32)
    for e in range(4):
        lines = jnp.where(lane == e, language_ref[e], lines)
    lang_send[...] = lines

    pl.semaphore_wait(barrier, jnp.where(diagonal, 20, 22))

    other = me.at(y=x, x=y)
    turn = pltpu.make_async_remote_copy(
        src_ref=turned.at[1], dst_ref=base, send_sem=turn_sem.at[0, 0], recv_sem=turn_sem.at[1, 0],
        device_id=other, device_id_type=MESH)

    def meanwhile():
        @pl.when(jnp.logical_not(diagonal))
        def _():
            turn.start()

        @pl.when(diagonal)
        def _():
            base[...] = turned[1]

        loads[0].wait()
        loads[1].wait()
        scale_columns(w_first, gain_ref, y * 10, 0, 10)

    lang_copies = [links.start(lang_send, lang_all.at[y], me.at(y=me.yo(k))) for k in (1, 2, 3)]

    finish_gather = gather_turned(
        links, me, blocks, turned.at[0], column, wide_send, wide_recv, meanwhile)

    ones = jnp.ones((8, 256), F32)

    def products(g):
        product = jnp.dot(w_first[...], blocks[g].reshape(SLICE, 256), preferred_element_type=F32)
        return product[:UNITS], product[UNITS:]

    def measure(g):
        wide = blocks[g, :, c].astype(F32).reshape(SLICE // 2, 256)
        squares[g] = ones * jnp.sum(wide * wide, axis=0, keepdims=True)

    up, down, far = me.yo(1), me.yo(-1), me.yo(2)
    to_up, to_down, to_far = me.at(y=up), me.at(y=down), me.at(y=far)
    gate, value = products(far)
    pre_send[far, 0] = gate.astype(BF16)
    relay_gate = links.start(pre_send.at[far, 0], relay_in.at[0], to_up)
    pre_send[far, 1] = value.astype(BF16)
    relay_value = links.start(pre_send.at[far, 1], relay_in.at[1], to_down)
    measure(far)
    square_copies = [links.start(squares.at[far], squares_in.at[0], to_far)]
    gate, value = products(up)
    pre_send[up, 0] = gate.astype(BF16)
    pre_send[up, 1] = value.astype(BF16)
    straight_up = links.start(pre_send.at[up, 1], pre_in.at[0, 1], to_up)
    measure(up)
    square_copies.append(links.start(squares.at[up], squares_in.at[1], to_up))
    gate, value = products(down)
    pre_send[down, 0] = gate.astype(BF16)
    straight_down = links.start(pre_send.at[down, 0], pre_in.at[1, 0], to_down)
    pre_send[down, 1] = value.astype(BF16)
    measure(down)
    square_copies.append(links.start(squares.at[down], squares_in.at[2], to_down))
    relay_gate.wait_recv()
    add_to(pre_send.at[up, 0], relay_in.at[0])
    joint_up = links.start(pre_send.at[up, 0], pre_in.at[0, 0], to_up)
    relay_value.wait_recv()
    add_to(pre_send.at[down, 1], relay_in.at[1])
    joint_down = links.start(pre_send.at[down, 1], pre_in.at[1, 1], to_down)
    gate, value = products(y)
    measure(y)
    pre_own[0] = gate
    pre_own[1] = value
    for copy in lang_copies:
        copy.wait_recv()
    lang_all[y] = lang_send[...]
    for g in range(4):
        names = lang_all[g].astype(F32)
        for e in range(4):
            name = jnp.max(jnp.where(lane == e, names, 0.0)).astype(jnp.int32)
            languages_ref[g * 4 + e] = name
    most = jnp.int32(0)
    for l in range(4):
        load = jnp.int32(0)
        for i in range(16):
            load = load + (languages_ref[i] == l).astype(jnp.int32)
        most = jnp.maximum(most, load)
    branch_ref[0] = (most > 4).astype(jnp.int32) + (most > 6).astype(jnp.int32)
    for copy in square_copies:
        copy.wait_recv()
    squares_core[0] = squares[y] + squares_in[0] + squares_in[1] + squares_in[2]
    core_square = links.start(squares_core.at[0], squares_core.at[1], me.at(c=1 - c))
    core_square.wait_recv()
    total = squares_core[0] + squares_core[1]
    inverse = lax.rsqrt(total * (1.0 / WIDTH) + EPS)[0:1, :]
    straight_up.wait_recv()
    straight_down.wait_recv()
    joint_up.wait_recv()
    joint_down.wait_recv()
    gate = (pre_own[0] + pre_in[0, 0].astype(F32) + pre_in[1, 0].astype(F32)) * inverse
    value = (pre_own[1] + pre_in[0, 1].astype(F32) + pre_in[1, 1].astype(F32)) * inverse
    hidden[y] = (gelu(gate) * value).astype(BF16)

    half = UNITS // 2
    low, high = pl.ds(0, half), pl.ds(half, half)

    def units(g, part, device):
        return links.start(hidden.at[g, part], hidden.at[g, part], device)

    low_up, high_down = units(y, low, to_up), units(y, high, to_down)
    high_up, low_down = units(y, high, to_up), units(y, low, to_down)
    loads[2].wait()
    partner = me.at(c=1 - c)
    core_copies = []

    def outward(g):
        sums[g] = contract(w_out[...], hidden[g]).astype(BF16).reshape(NZ, 2, PART, 256)
        core_copies.append((g, links.start(sums.at[g, :, 1 - c], theirs.at[g], partner)))

    def join():
        g, copy = core_copies.pop(0)
        copy.wait_recv()
        add_to(sums.at[g, :, c], theirs.at[g])

    outward(y)
    low_up.wait_recv()
    far_up = units(down, low, to_up)
    high_down.wait_recv()
    far_down = units(up, high, to_down)
    high_up.wait_recv()
    outward(down)
    low_down.wait_recv()
    outward(up)
    for _ in range(3):
        join()
    far_up.wait_recv()
    far_down.wait_recv()
    outward(far)

    scatter_plane(
        links, me,
        (sums, theirs, cross_in, along_in, tail_along_in, tail_cross_in, result),
        core_copies,
    )

    @pl.when(jnp.logical_not(diagonal))
    def _():
        turn.wait_recv()

    encoded = (blocks[x, z, c].astype(F32) + result[...]).astype(BF16)
    baseline = base[...].astype(F32)
    difference = encoded.astype(F32) - baseline
    example = lax.broadcasted_iota(jnp.int32, (PART, 256), 1) // SEQ
    size = jnp.abs(difference)
    scale = jnp.zeros((PART, 256), F32)
    for e in range(4):
        top = jnp.max(jnp.where(example == e, size, 0.0), axis=1, keepdims=True) + EPS
        scale = jnp.where(example == e, top, scale)
    codes = (difference / scale).astype(BF16)
    memory = (baseline + codes.astype(F32) * scale).astype(BF16)
    pair_ref[0] = memory
    pair_ref[1] = codes

    slot_lane = lax.broadcasted_iota(jnp.int32, (SEQ, PAIR), 1)
    slot_line = lax.broadcasted_iota(jnp.int32, (SEQ, PAIR), 0)
    for l in range(4):
        count, picks = jnp.int32(0), []
        for e in range(4):
            named = languages_ref[x * 4 + e] == l
            start = jnp.where(named, count * SEQ, -SEQ)
            count = count + named.astype(jnp.int32)
            picks.append((slot_lane == slot_line + start).astype(F32).astype(BF16))
        picked = jnp.dot(memory, jnp.concatenate(picks, axis=0), preferred_element_type=F32)
        fan_out[l] = picked.astype(BF16)

    def fan_copy(l, g):
        return pltpu.make_async_remote_copy(
            src_ref=fan_out.at[l], dst_ref=memory_all.at[g], send_sem=fan_send.at[l], recv_sem=fan_recv.at[g],
            device_id=me.at(y=l, x=y), device_id_type=MESH)

    fans = [fan_copy(l, x) for l in range(4)]
    arrivals = [fan_copy(g, g) for g in range(4)]
    for l in range(4):
        @pl.when(jnp.logical_not(jnp.logical_and(diagonal, y == l)))
        def _():
            fans[l].start()

    @pl.when(diagonal)
    def _():
        memory_all[x] = fan_out[y]

    for g in range(4):
        @pl.when(jnp.logical_not(jnp.logical_and(diagonal, x == g)))
        def _():
            arrivals[g].wait_recv()

    all_ref[...] = memory_all[...]

    for l in range(4):
        @pl.when(jnp.logical_not(jnp.logical_and(diagonal, y == l)))
        def _():
            fans[l].wait_send()

    @pl.when(jnp.logical_not(diagonal))
    def _():
        turn.wait_send()

    finish_gather()
    links.finish()


def decoder_kernel(
    rows, memory_ref, pair_ref, language_ref, gain_ref, gate_hbm, in_hbm, out_hbm,
    decoded_ref, new_memory_ref, quantized_ref,
    blocks, own, w_first, w_out, hidden, acc, squares, finished, home,
    sums, theirs, cross_in, along_in, tail_along_in, tail_cross_in, result,
    send_sem, recv_sem, turn_sem, load_sem,
):
    me = Place()
    x, y, z, c = me.x, me.y, me.z, me.c
    links = Links(send_sem, recv_sem)
    diagonal = x == y
    other = me.at(y=x, x=y)

    def greet_other(barrier):
        @pl.when(jnp.logical_not(diagonal))
        def _():
            pl.semaphore_signal(barrier, inc=1, device_id=other, device_id_type=MESH)

    barrier = greet(me.plane() + me.column(), greet_other)
    loads = [
        pltpu.make_async_copy(src, dst, load_sem.at[i])
        for i, (src, dst) in enumerate(first_weights(w_first, gate_hbm, in_hbm) + [(out_hbm, w_out)])
    ]
    for load in loads:
        load.start()

    lane = lax.broadcasted_iota(jnp.int32, (SEQ, rows), 1)
    line = lax.broadcasted_iota(jnp.int32, (SEQ, rows), 0)
    number = jnp.int32(0)
    chosen = jnp.zeros((PART, rows), F32)
    for g in range(4):
        count = jnp.int32(0)
        for e in range(4):
            count = count + (language_ref[g * 4 + e] == y).astype(jnp.int32)
        picks = []
        for j in range(2):
            start = jnp.where(count > j, (number + j) * SEQ, -SEQ)
            picks.append((lane == line + start).astype(F32).astype(BF16))
        number = number + count
        chosen = chosen + jnp.dot(memory_ref[g], jnp.concatenate(picks, axis=0), preferred_element_type=F32)
    own[...] = chosen.astype(BF16)
    blocks[x, z, c] = own[...]

    pl.semaphore_wait(barrier, jnp.where(diagonal, 14, 15))

    turn = pltpu.make_async_remote_copy(
        src_ref=pair_ref, dst_ref=home, send_sem=turn_sem.at[0], recv_sem=turn_sem.at[1],
        device_id=other, device_id_type=MESH)

    def meanwhile(i):
        if i == 0:
            @pl.when(jnp.logical_not(diagonal))
            def _():
                turn.start()

            @pl.when(diagonal)
            def _():
                home[...] = pair_ref[...]

            loads[0].wait()
            loads[1].wait()
        scale_columns(w_first, gain_ref, 0, 5 * i, 5)

    squares[0] = jnp.zeros((8, rows), F32)

    def seen(ref):
        wide = ref[...].astype(F32)
        squares[0] = squares[0] + jnp.sum(wide * wide, axis=(0, 1))[None, :]

    gather_plane(links, me, blocks, meanwhile, seen)
    partner = me.at(c=1 - c)
    core_square = links.start(squares.at[0], squares.at[1], partner)
    for g in range(4):
        part = pl.ds(g * SLICE, SLICE)
        term = jnp.dot(w_first[:, part], blocks[g].reshape(SLICE, rows), preferred_element_type=F32)
        acc[...] = term if g == 0 else acc[...] + term
    core_square.wait_recv()
    inverse = lax.rsqrt((squares[0] + squares[1]) * (1.0 / WIDTH) + EPS)[0:1, :]
    hidden[...] = (gelu(acc[:UNITS] * inverse) * (acc[UNITS:] * inverse)).astype(BF16)

    loads[2].wait()
    core_copies = []
    for k in (2, 1, 3, 0):
        g = me.xo(k)
        columns = pl.ds(pl.multiple_of(g * SLICE, 128), SLICE)
        product = contract(w_out[:, columns], hidden[...])
        sums[g] = product.astype(BF16).reshape(NZ, 2, PART, rows)
        core_copies.append((g, links.start(sums.at[g, :, 1 - c], theirs.at[g], partner)))
    scatter_plane(
        links, me,
        (sums, theirs, cross_in, along_in, tail_along_in, tail_cross_in, result),
        core_copies,
    )
    finished[y] = (own[...].astype(F32) + result[...]).astype(BF16)
    returns = [links.start(finished.at[y], finished.at[y], me.at(y=me.yo(k))) for k in (1, 2, 3)]

    place = lax.broadcasted_iota(jnp.int32, (rows, 256), 0)
    column = lax.broadcasted_iota(jnp.int32, (rows, 256), 1)
    example, token = column // SEQ, column % SEQ
    sources = []
    for l in range(4):
        source = jnp.full((rows, 256), -1, jnp.int32)
        for e in range(4):
            lang = language_ref[y * 4 + e]
            slot = jnp.int32(0)
            for i in range(16):
                ahead = jnp.logical_and(language_ref[i] == lang, i < y * 4 + e)
                slot = slot + ahead.astype(jnp.int32)
            start = jnp.where(lang == l, slot * SEQ, -SEQ)
            source = jnp.where(example == e, token + start, source)
        sources.append((place == source).astype(F32).astype(BF16))

    @pl.when(jnp.logical_not(diagonal))
    def _():
        turn.wait_recv()

    new_memory_ref[...] = home[0].T.reshape(4, SEQ, PART)
    quantized_ref[...] = home[1].T.reshape(4, SEQ, PART)
    for copy in returns:
        copy.wait_recv()
    answer = jnp.zeros((PART, 256), F32)
    for l in range(4):
        answer = answer + jnp.dot(finished[l], sources[l], preferred_element_type=F32)
    decoded_ref[...] = answer.astype(BF16).T.reshape(4, SEQ, PART)

    @pl.when(jnp.logical_not(diagonal))
    def _():
        turn.wait_send()

    links.finish()


VMEM = pl.BlockSpec(memory_space=pltpu.VMEM)
SMEM = pl.BlockSpec(memory_space=pltpu.SMEM)
ANY = pl.BlockSpec(memory_space=pl.ANY)
DMA = pltpu.SemaphoreType.DMA


def encode(tokens, history, ids, language, gain, gate, up, out):
    sds = jax.ShapeDtypeStruct
    return pl.pallas_call(
        encoder_kernel,
        out_shape=(
            sds((4, PART, PAIR), BF16),
            sds((2, PART, 256), BF16),
            sds((16,), jnp.int32),
            sds((1,), jnp.int32),
        ),
        in_specs=[VMEM, VMEM, SMEM, SMEM, VMEM, ANY, ANY, ANY],
        out_specs=(VMEM, VMEM, SMEM, SMEM),
        scratch_shapes=[
            pltpu.VMEM((2, PART, 256), BF16),
            pltpu.VMEM((NZ, TURN_HEAD, 256), BF16),
            pltpu.VMEM((PART, 256), BF16),
            pltpu.VMEM((NX, NZ, 2, PART, 256), BF16),
            pltpu.VMEM((2 * UNITS, SLICE), BF16),
            pltpu.VMEM((UNITS, SLICE), BF16),
            pltpu.VMEM((4, 2, UNITS, 256), BF16),
            pltpu.VMEM((2, UNITS, 256), BF16),
            pltpu.VMEM((2, 2, UNITS, 256), BF16),
            pltpu.VMEM((2, UNITS, 256), F32),
            pltpu.VMEM((4, 8, 256), F32),
            pltpu.VMEM((3, 8, 256), F32),
            pltpu.VMEM((2, 8, 256), F32),
            pltpu.VMEM((4, UNITS, 256), BF16),
            pltpu.VMEM((8, 128), jnp.int32),
            pltpu.VMEM((4, PART, PAIR), BF16),
            pltpu.VMEM((4, PART, PAIR), BF16),
            pltpu.VMEM((4, 8, 128), jnp.int32),
            *scatter_shapes(256),
            DMA((COPIES,)),
            DMA((COPIES,)),
            DMA((2, 1)),
            DMA((9, 4)),
            DMA((9, 4)),
            DMA((4,)),
            DMA((4,)),
            DMA((3,)),
        ],
        compiler_params=pltpu.CompilerParams(
            collective_id=0, has_side_effects=True, vmem_limit_bytes=56 << 20
        ),
    )(tokens, history, ids, language, gain, gate, up, out)


def decode(rows, number, memory, pair, language, gain, gate, up, out):
    return pl.pallas_call(
        functools.partial(decoder_kernel, rows),
        out_shape=(jax.ShapeDtypeStruct((4, SEQ, PART), BF16),) * 3,
        in_specs=[VMEM, VMEM, SMEM, VMEM, ANY, ANY, ANY],
        out_specs=(VMEM, VMEM, VMEM),
        scratch_shapes=[
            pltpu.VMEM((NX, NZ, 2, PART, rows), BF16),
            pltpu.VMEM((PART, rows), BF16),
            pltpu.VMEM((2 * UNITS, WIDTH), BF16),
            pltpu.VMEM((UNITS, WIDTH), BF16),
            pltpu.VMEM((UNITS, rows), BF16),
            pltpu.VMEM((2 * UNITS, rows), F32),
            pltpu.VMEM((2, 8, rows), F32),
            pltpu.VMEM((4, PART, rows), BF16),
            pltpu.VMEM((2, PART, 256), BF16),
            *scatter_shapes(rows),
            DMA((COPIES,)),
            DMA((COPIES,)),
            DMA((2,)),
            DMA((3,)),
        ],
        compiler_params=pltpu.CompilerParams(
            collective_id=number, has_side_effects=True, vmem_limit_bytes=56 << 20
        ),
    )(memory, pair, language, gain, gate, up, out)


def shards(
    tokens, language, example_ids, history, enc_gain, dec_gain, enc_gate, enc_in, enc_out, dec_gate, dec_in, dec_out
):
    memory_all, pair, languages, branch = encode(
        tokens, history, example_ids, language.reshape(4), enc_gain.reshape(40, 128), enc_gate.T, enc_in.T, enc_out
    )
    return lax.switch(
        branch[0],
        [functools.partial(decode, rows * SEQ, number) for number, rows in ((1, 4), (2, 6), (3, 8))],
        memory_all, pair, languages, dec_gain.reshape(40, 128), dec_gate[0].T, dec_in[0].T, dec_out[0],
    )


def solution(mesh):
    in_specs = (
        P("section", None, "tp"),
        P("section", None),
        P("section"),
        P(None, None, "tp"),
        P(),
        P("section", None),
        P("section", "tp"),
        P("section", "tp"),
        P("tp", "section"),
        P("section", None, "tp"),
        P("section", None, "tp"),
        P("section", "tp", None),
    )
    out_specs = (P("section", None, "tp"), P("section", None, "tp"), P("section", None, "tp"))
    return jax.shard_map(shards, mesh=mesh, in_specs=in_specs, out_specs=out_specs, check_vma=False)
```
